256 devices in a mesh: seq: 64 (over z, x_lo, y), ch: 4 (over x_hi, core).
Axes of the slice: x: 4 (x_hi: 2, x_lo: 2; x = x_hi * 2 + x_lo), y: 4, z: 8, core: 2. Of those that a mesh axis runs over, the one named last changes fastest.
Arguments:
- tokens: bfloat16 [8192, 2048], P('seq'), may hold values from -16 to 16
- value_weight: bfloat16 [2048, 2048], P(None, 'ch'), may hold values from -0.125 to 0.125
- gate_weight: bfloat16 [2048, 2048], P(None, 'ch'), may hold values from -0.125 to 0.125
- filters: float32 [8192, 2048], P('seq', 'ch'), may hold values from -0.0625 to 0.0625
- cotangent: bfloat16 [8192, 2048], P('seq', 'ch'), may hold values from -6 to 6
Outputs:
- input_grad: bfloat16 [8192, 2048], P('seq', 'ch')
- filter_grad: float32 [8192, 2048], P('seq', 'ch')
- value_weight_grad: float32 [2048, 2048], P('seq', 'ch')
- gate_weight_grad: float32 [2048, 2048], P('seq', 'ch')
The draws below stay inside these ranges and needn't reach their ends.
All inputs are finite; a program needn't handle non-finite values.
Results may differ from the reference program's by a relative error of at most 0.0049.
Values may be sent and summed in bfloat16 or wider, within the bound.
A program may use at most 128 MiB of HBM per device.

```python
import jax
import jax.numpy as jnp

D = 2048
WIN = 2048
SEQ = 8192


def raised(drawn, key, source, target, blocks, factor):
    owner, partner = [(jnp.arange(drawn.shape[dim]) // (drawn.shape[dim] // blocks)).reshape([-1 if axis == dim else 1 for axis in range(drawn.ndim)]) for dim in (source, target)]
    chosen = jax.random.permutation(key, blocks)[partner]
    strong = (owner == chosen) | (owner == (partner + blocks // 2) % blocks)
    return jnp.where(strong, factor * drawn, drawn)


def block_levels(own_key, shape, shards, low, high):
    gain, own = 1.0, jax.random.fold_in(own_key, 6)
    for position, parts in shards:
        heights = jnp.exp(jax.random.uniform(jax.random.fold_in(own, position), (parts,), jnp.float32, low / len(shards), high / len(shards)))
        gain = gain * jnp.repeat(heights, shape[position] // parts).reshape([-1 if axis == position else 1 for axis in range(len(shape))])
    return gain


def scatter_about(rng, extent, scale, reach, split=(), held_as=jnp.bfloat16):
    entries = jax.random.normal(rng, extent, jnp.float32) * scale
    if len(split) > 0:
        entries = block_levels(rng, extent, split, -0.22, 0.18) * entries
    return jnp.clip(entries, min=-reach, max=reach).astype(held_as)


def bell_draw_with(rng, dims, scale, most, cuts, heavy, dtype=jnp.bfloat16):
    values = scale * jax.random.normal(rng, dims, jnp.float32)
    if cuts:
        values = values * block_levels(rng, dims, cuts, -0.22, 0.18)
    return jnp.clip(raised(values, jax.random.fold_in(rng, 3), *heavy), -most, most).astype(dtype)


def setup_inputs(seed: int = 0) -> dict:
    seeds = jax.random.split(jax.random.key(seed), 6)
    return {
        "tokens": bell_draw_with(seeds[0], (SEQ, D), 1.0, 16.0, ((0, 64),), (0, 1, 64, 4.0)),
        "value_weight": scatter_about(seeds[1], (D, WIN), D ** -0.5, 0.125, ((1, 4),)),
        "gate_weight": scatter_about(seeds[2], (D, WIN), D ** -0.5, 0.125, ((1, 4),)),
        "filters": scatter_about(seeds[3], (SEQ, WIN), SEQ ** -0.5, 0.0625, ((0, 64), (1, 4)), jnp.float32),
        "cotangent": scatter_about(seeds[4], (SEQ, WIN), 1.0, 6.0, ((0, 64), (1, 4))),
    }


def reference(tokens, value_weight, gate_weight, filters, cotangent):
    padded = 2 * SEQ
    tok_full = tokens.astype(jnp.float32)
    values = jnp.dot(tok_full, value_weight.astype(jnp.float32), preferred_element_type=jnp.float32)
    gating = jnp.dot(tok_full, gate_weight.astype(jnp.float32), preferred_element_type=jnp.float32)
    cot_full = cotangent.astype(jnp.float32)
    upstream = cot_full * gating
    value_hat = jnp.fft.rfft(values, n=padded, axis=0)
    filter_hat = jnp.fft.rfft(filters, n=padded, axis=0)
    upstream_hat = jnp.fft.rfft(upstream, n=padded, axis=0)
    conv_out = jnp.fft.irfft(value_hat * filter_hat, n=padded, axis=0)[:SEQ]
    value_raw = jnp.fft.irfft(jnp.conj(filter_hat) * upstream_hat, n=padded, axis=0)[:SEQ]
    filter_raw = jnp.fft.irfft(jnp.conj(value_hat) * upstream_hat, n=padded, axis=0)[:SEQ]
    grad_scale = SEQ ** -0.5
    value_grad = value_raw.astype(jnp.bfloat16)
    gate_grad = (cot_full * conv_out).astype(jnp.bfloat16)
    filter_grad = filter_raw * grad_scale
    vgrad_full = value_grad.astype(jnp.float32)
    ggrad_full = gate_grad.astype(jnp.float32)
    value_weight_grad = jnp.dot(tok_full.T, vgrad_full, preferred_element_type=jnp.float32) * grad_scale
    gate_weight_grad = jnp.dot(tok_full.T, ggrad_full, preferred_element_type=jnp.float32) * grad_scale
    input_grad = (jnp.dot(vgrad_full, value_weight.astype(jnp.float32).T, preferred_element_type=jnp.float32)
                  + jnp.dot(ggrad_full, gate_weight.astype(jnp.float32).T, preferred_element_type=jnp.float32)).astype(jnp.bfloat16)
    return input_grad, filter_grad, value_weight_grad, gate_weight_grad
```

```python
import functools
import math

import jax
import jax.numpy as jnp
import ml_dtypes
import numpy as np
from jax import lax
from jax.experimental import pallas as pl
from jax.experimental.pallas import tpu as pltpu
from jax.sharding import PartitionSpec as P

MESH = pl.DeviceIdType.MESH
F32 = jnp.float32
BF16 = jnp.bfloat16
SIDE = 128
PADDED = SIDE * SIDE
SEQ = PADDED // 2
SCALE = SEQ**-0.5
ORDER = (4, 3, 5, 2, 6, 1, 7)


def split(table):
    high = table.astype(ml_dtypes.bfloat16)
    low = (table - high.astype(np.float64)).astype(ml_dtypes.bfloat16)
    return high, low


def tables():
    half = np.arange(64) + 0.5
    block = 2 * math.pi * np.outer(half, np.arange(64)) / SIDE
    first = np.concatenate([np.cos(block), -np.sin(block)], axis=0)
    first = np.concatenate(split(first), axis=1)
    twist = 2 * math.pi * np.outer(half, np.arange(SIDE)) / PADDED
    twist = np.concatenate([np.cos(twist), np.sin(twist)], axis=0).astype(np.float32)
    inner = 2 * math.pi * np.outer(np.arange(SIDE), np.arange(SIDE)) / SIDE
    c, s = np.cos(inner), np.sin(inner)
    forward = np.block([[c, -s], [s, c]])
    inverse = np.block([[c, s], [-s, c]])
    second = np.concatenate(split(forward) + split(inverse), axis=0)
    last = np.concatenate([np.cos(block.T), -np.sin(block.T)], axis=1) * (2.0 / PADDED)
    high, low = split(last)
    last = np.concatenate([high, high, low], axis=1)
    return first, twist, second, last


def dot(a, b):
    return jnp.dot(a, b, preferred_element_type=F32)


def halves(x):
    high = x.astype(BF16)
    return high, (x - high.astype(F32)).astype(BF16)


def kernel(
    tok, vw, gw, fil, cot, t_first, t_twist, t_second, t_last,
    input_grad, filter_grad, vw_grad, gw_grad,
    s_e, s_l, r1_e, r1_l, r2_e, r2_l, u_e, u_l, w_vg, w_f,
    spec, lhs, mid, s3, r3, r3s, r4, s3f, r3f, s4f, r4f,
    tk, g_all, part, r5, s6, r6, vt, gt, s7, r7, s8, r8,
    sem_qe, sem_ql, sem_ze, sem_zl, sem_zv, sem_zf, sem_qv, sem_qf, sem_q6,
    sem_tk, sem_sib, sem_rs, sem_c7, sem_x8, sem_own,
):
    i = lax.axis_index("seq")
    c = lax.axis_index("ch")
    z, q = i // 8, i % 8
    core, xh = c % 2, c // 2
    sib = c + 1 - 2 * core
    opp = (c + 2) % 4

    def along_z(zz):
        return (zz * 8 + q, c)

    def along_q(qq):
        return (z * 8 + qq, c)

    barrier = pltpu.get_barrier_semaphore()
    peers = 0
    for d in range(1, 8):
        for who in (along_z((z + d) % 8), along_q((q + d) % 8), (((z + d) % 8) * 8 + q, sib)):
            pl.semaphore_signal(barrier, inc=1, device_id=who, device_id_type=MESH)
            peers += 1
    for who in ((i, sib), (i, opp)):
        pl.semaphore_signal(barrier, inc=1, device_id=who, device_id_type=MESH)
        peers += 1

    def pair(a, b):
        a = a.T.reshape(16, 8, SIDE)
        b = b.T.reshape(16, 8, SIDE)
        return jnp.concatenate([a, b], axis=1).astype(BF16).reshape(2, SIDE, SIDE)

    pending = []

    def send(src, dst, ssem, rsem, who):
        copy = pltpu.make_async_remote_copy(
            src_ref=src, dst_ref=dst, send_sem=ssem, recv_sem=rsem, device_id=who, device_id_type=MESH
        )
        copy.start()
        pending.append(copy)

    def arrived(dst, sem, who):
        pltpu.make_async_remote_copy(
            src_ref=dst, dst_ref=dst, send_sem=sem.at[0, 0], recv_sem=sem.at[1, who],
            device_id=(i, sib), device_id_type=MESH,
        ).wait_recv()

    def exchange(me, reach, source, landing, sem):
        for d in ORDER:
            peer = (me + d) % 8
            send(source(peer), landing(me), sem.at[0, d], sem.at[1, me], reach(peer))

    def collect(me, landing, sem):
        for d in ORDER:
            peer = (me + d) % 8
            arrived(landing(peer), sem, peer)

    def rows16(ref, at):
        return ref.at[:, pl.ds(pl.multiple_of(at * 16, 16), 16), :]

    for b in range(4):
        lanes = slice(b * SIDE, (b + 1) * SIDE)
        s_e[2 * b : 2 * b + 2] = pair(fil[:, lanes], cot[:, lanes].astype(F32))
    own_cols = pl.ds(pl.multiple_of(core * 1024, 1024), 1024)
    own = pltpu.make_async_copy(tok.at[:, own_cols], tk.at[q], sem_own)
    own.start()

    pl.semaphore_wait(barrier, peers)
    exchange(q, along_q, lambda p: s_e.at[p], lambda p: r1_e.at[p], sem_qe)
    r1_e[pl.ds(q, 1)] = s_e[pl.ds(q, 1)]

    for b in range(2):
        lanes = slice(b * 256, (b + 1) * 256)
        val = dot(tok[...], vw[:, lanes])
        up = dot(tok[...], gw[:, lanes]) * cot[:, lanes].astype(F32)
        for e in range(2):
            part_lanes = slice(e * SIDE, (e + 1) * SIDE)
            at = 4 * b + 2 * e
            s_l[at : at + 2] = pair(val[:, part_lanes], up[:, part_lanes])
    exchange(q, along_q, lambda p: s_l.at[p], lambda p: r1_l.at[p], sem_ql)
    r1_l[pl.ds(q, 1)] = s_l[pl.ds(q, 1)]

    def second_phase(r1, r2, sem_q, sem_z):
        collect(q, lambda p: r1.at[p], sem_q)
        exchange(z, along_z, lambda p: rows16(r1, p), lambda p: r2.at[p], sem_z)
        mine = r1[:, pl.ds(pl.multiple_of(z * 16, 16), 16), :]
        r2[pl.ds(z, 1)] = mine.reshape(1, 8, 16, SIDE)

    second_phase(r1_e, r2_e, sem_qe, sem_ze)
    for d in ORDER:
        peer = (q + d) % 8
        send(tok.at[:, own_cols], tk.at[q], sem_tk.at[0, d], sem_tk.at[1, q], along_q(peer))
    second_phase(r1_l, r2_l, sem_ql, sem_zl)

    cw = t_twist[0:64]
    sw = t_twist[64:128]
    g_high, g_low, i_high, i_low = (t_second[256 * t : 256 * (t + 1)] for t in range(4))

    def put(at, x):
        high, low = halves(x)
        lhs[0, at * 64 : (at + 1) * 64] = high
        lhs[1, at * 64 : (at + 1) * 64] = low

    def widen(r2, u):
        for zz in range(8):
            u[zz * SIDE : (zz + 1) * SIDE] = r2[zz].reshape(SIDE, SIDE).astype(F32)

    def forward(u, base, out):
        for r in range(0, 8, 2):
            x = [u[pl.ds(base + r + e, 64, stride=16), :] for e in range(2)]
            x = jnp.concatenate(x, axis=1).astype(BF16)
            a = dot(t_first[...], jnp.concatenate([x, x], axis=0))
            for e in range(2):
                re = a[:64, e * SIDE : (e + 1) * SIDE]
                im = a[64:, e * SIDE : (e + 1) * SIDE]
                put(r + e, jnp.concatenate([re * cw + im * sw, im * cw - re * sw], axis=1))
        spec[out] = dot(lhs[0], g_high) + (dot(lhs[1], g_high) + dot(lhs[0], g_low))

    def inverse(left, right, conjugate, store):
        for r in range(8):
            rows = slice(r * 64, (r + 1) * 64)
            ar, ai = spec[left, rows, :SIDE], spec[left, rows, SIDE:]
            br, bi = spec[right, rows, :SIDE], spec[right, rows, SIDE:]
            if conjugate:
                p = [ar * br + ai * bi, ar * bi - ai * br]
            else:
                p = [ar * br - ai * bi, ar * bi + ai * br]
            put(r, jnp.concatenate(p, axis=1))
        mid[...] = dot(lhs[0], i_high) + (dot(lhs[1], i_high) + dot(lhs[0], i_low))
        for r in range(0, 8, 2):
            cols = []
            for e in range(2):
                rows = slice((r + e) * 64, (r + e + 1) * 64)
                re, im = mid[rows, :SIDE], mid[rows, SIDE:]
                cols.append(jnp.concatenate([re * cw - im * sw, im * cw + re * sw], axis=0))
            high, low = halves(jnp.concatenate(cols, axis=1))
            y = dot(t_last[...], jnp.concatenate([high, low, high], axis=0))
            for e in range(2):
                store(r + e, y[:, e * SIDE : (e + 1) * SIDE])

    collect(z, lambda p: r2_e.at[p], sem_ze)
    widen(r2_e, u_e)
    forward(u_e, 0, 0)
    collect(z, lambda p: r2_l.at[p], sem_zl)
    widen(r2_l, u_l)
    forward(u_l, 8, 2)
    forward(u_l, 0, 1)

    def store_v(r, y):
        w_vg[pl.ds(r, 64, stride=16), :] = y

    def store_g(r, y):
        w_vg[pl.ds(8 + r, 64, stride=16), :] = y * u_e[pl.ds(8 + r, 64, stride=16), :]

    def store_f(r, y):
        w_f[pl.ds(r, 64, stride=8), :] = y

    inverse(0, 2, True, store_v)
    inverse(0, 1, False, store_g)
    for zz in range(8):
        s3[zz] = w_vg[zz * SIDE : (zz + 1) * SIDE].astype(BF16)
    exchange(z, along_z, lambda p: s3.at[p], lambda p: r3.at[p], sem_zv)
    r3[pl.ds(z, 1)] = s3[pl.ds(z, 1)]
    inverse(1, 2, True, store_f)
    for zz in range(8):
        s3f[zz] = w_f[zz * 64 : (zz + 1) * 64].astype(BF16)
    exchange(z, along_z, lambda p: s3f.at[p], lambda p: r3f.at[p], sem_zf)
    r3f[pl.ds(z, 1)] = s3f[pl.ds(z, 1)]

    send(r3.at[z], r3s.at[z], sem_sib.at[0, 0], sem_sib.at[1, z], (i, sib))
    for d in ORDER:
        peer = (z + d) % 8
        arrived(r3.at[peer], sem_zv, peer)
        send(r3.at[peer], r3s.at[peer], sem_sib.at[0, d], sem_sib.at[1, peer], (i, sib))
    exchange(q, along_q, lambda p: rows16(r3, p), lambda p: r4.at[p], sem_qv)
    r4[pl.ds(q, 1)] = r3[:, pl.ds(pl.multiple_of(q * 16, 16), 16), :].reshape(1, 8, 16, SIDE)

    collect(q, lambda p: tk.at[p], sem_tk)
    own.wait()
    for qq in range(8):
        g_all[0:SIDE, qq * SIDE : (qq + 1) * SIDE] = r3[:, qq * 16 : (qq + 1) * 16, :].reshape(SIDE, SIDE)
    for d in ORDER + (0,):
        arrived(r3s.at[(z + d) % 8], sem_sib, (z + d) % 8)
    for qq in range(8):
        g_all[SIDE:, qq * SIDE : (qq + 1) * SIDE] = r3s[:, qq * 16 : (qq + 1) * 16, :].reshape(SIDE, SIDE)
    for t in range(4):
        block = tk[:, :, t * 256 : (t + 1) * 256].reshape(1024, 256)
        sums = dot(g_all[...], block).astype(BF16)
        part[t, 0] = sums[:SIDE]
        part[t, 1] = sums[SIDE:]
        to = core * 4 + t

        def share(s, who, t=t, to=to):
            return pltpu.make_async_remote_copy(
                src_ref=part.at[t, s], dst_ref=r5.at[z], send_sem=sem_rs.at[0, 2 * t + s],
                recv_sem=sem_rs.at[1, z], device_id=(to * 8 + q, who), device_id_type=MESH,
            )

        share(1, sib).start()

        @pl.when(to != z)
        def _():
            share(0, c).start()

        @pl.when(to == z)
        def _():
            r5[pl.ds(z, 1)] = part[t, 0].reshape(1, SIDE, 256)

    collect(q, lambda p: r4.at[p], sem_qv)
    for qq in range(8):
        x = r4[qq].astype(F32)
        vt[:, qq * 64 : (qq + 1) * 64] = x[:, :8].reshape(64, SIDE).T.astype(BF16)
        gt[:, qq * 64 : (qq + 1) * 64] = x[:, 8:].reshape(64, SIDE).T.astype(BF16)

    def columns(k):
        rows = pl.ds(pl.multiple_of(k * 512, 512), 512)
        over = (((1,), (1,)), ((), ()))
        a = lax.dot_general(vt[...], vw[rows, :], over, preferred_element_type=F32)
        return a + lax.dot_general(gt[...], gw[rows, :], over, preferred_element_type=F32)

    s7[0] = columns(2 * (1 - xh) + 1 - core)
    s7[1] = columns(2 * xh + 1 - core)
    send(s7, r7, sem_c7.at[0, 0], sem_c7.at[1, 0], (i, sib))
    far = columns(2 * (1 - xh) + core)
    near = columns(2 * xh + core)
    arrived(r7, sem_c7, 0)
    s8[...] = (far + r7[0]).astype(BF16)
    send(s8, r8, sem_x8.at[0, 0], sem_x8.at[1, 0], (i, opp))
    near = near + r7[1]

    collect(z, lambda p: r3f.at[p], sem_zf)
    x = r3f[...].astype(F32).reshape(8, 8, 8, SIDE)
    for qq in range(8):
        s4f[qq] = x[:, qq].reshape(64, SIDE).astype(BF16)
    exchange(q, along_q, lambda p: s4f.at[p], lambda p: r4f.at[p], sem_qf)
    r4f[pl.ds(q, 1)] = s4f[pl.ds(q, 1)]

    for d in ORDER:
        peer = (z + d) % 8
        arrived(r5.at[peer], sem_rs, peer)

    @pl.when(core != z // 4)
    def _():
        arrived(r5.at[z], sem_rs, z)

    total = r5[0].astype(F32)
    for zz in range(1, 8):
        total = total + r5[zz].astype(F32)
    total = total.reshape(8, 2, 8, 256)
    total = jnp.concatenate([total[:, 0].reshape(64, 256), total[:, 1].reshape(64, 256)], axis=0)
    s6[...] = (total.T * SCALE).reshape(8, 32, SIDE)
    exchange(q, along_q, lambda p: s6.at[p], lambda p: r6.at[p], sem_q6)
    r6[pl.ds(q, 1)] = s6[pl.ds(q, 1)]

    arrived(r8, sem_x8, 0)
    input_grad[...] = (near + r8[...].astype(F32)).astype(BF16)

    collect(q, lambda p: r4f.at[p], sem_qf)
    for b in range(4):
        x = r4f[2 * b : 2 * b + 2].astype(F32).reshape(SIDE, SIDE)
        filter_grad[:, b * SIDE : (b + 1) * SIDE] = x.T * SCALE

    collect(q, lambda p: r6.at[p], sem_q6)
    for qq in range(8):
        vw_grad[:, qq * 64 : (qq + 1) * 64] = r6[qq, :, :64]
        gw_grad[:, qq * 64 : (qq + 1) * 64] = r6[qq, :, 64:]

    for copy in pending:
        copy.wait_send()
    for t in range(4):
        for s in range(2):
            copy = pltpu.make_async_remote_copy(
                src_ref=part.at[t, s], dst_ref=r5.at[z], send_sem=sem_rs.at[0, 2 * t + s],
                recv_sem=sem_rs.at[1, z], device_id=(i, sib), device_id_type=MESH,
            )
            if s == 1:
                copy.wait_send()
            else:

                @pl.when(core * 4 + t != z)
                def _(copy=copy):
                    copy.wait_send()


def local(tokens, value_weight, gate_weight, filters, cotangent):
    def v(*shape, dtype=BF16):
        return pltpu.VMEM(shape, dtype)

    sem = pltpu.SemaphoreType.DMA((2, 8))
    vmem = pl.BlockSpec(memory_space=pltpu.VMEM)
    shape = jax.ShapeDtypeStruct
    return pl.pallas_call(
        kernel,
        out_shape=(
            shape((128, 512), BF16),
            shape((128, 512), F32),
            shape((32, 512), F32),
            shape((32, 512), F32),
        ),
        in_specs=[vmem] * 9,
        out_specs=(vmem,) * 4,
        scratch_shapes=[
            v(8, 128, 128), v(8, 128, 128), v(8, 128, 128), v(8, 128, 128),
            v(8, 8, 16, 128), v(8, 8, 16, 128),
            v(1024, 128, dtype=F32), v(1024, 128, dtype=F32), v(1024, 128, dtype=F32), v(512, 128, dtype=F32),
            v(3, 512, 256, dtype=F32), v(2, 512, 256), v(512, 256, dtype=F32),
            v(8, 128, 128), v(8, 128, 128), v(8, 128, 128), v(8, 8, 16, 128),
            v(8, 64, 128), v(8, 64, 128), v(8, 64, 128), v(8, 64, 128),
            v(8, 128, 1024), v(256, 1024), v(4, 2, 128, 256), v(8, 128, 256),
            v(8, 32, 128, dtype=F32), v(8, 32, 128, dtype=F32),
            v(128, 512), v(128, 512),
            v(2, 128, 512, dtype=F32), v(2, 128, 512, dtype=F32), v(128, 512), v(128, 512),
        ] + [sem] * 14 + [pltpu.SemaphoreType.DMA],
        compiler_params=pltpu.CompilerParams(
            collective_id=0, has_side_effects=True, vmem_limit_bytes=48 * 1024 * 1024
        ),
        cost_estimate=pl.CostEstimate(flops=3_000_000_000, bytes_accessed=8_000_000, transcendentals=0),
    )(tokens, value_weight, gate_weight, filters, cotangent, *(jnp.asarray(t) for t in tables()))


def solution(mesh):
    placed = (P("seq", None), P(None, "ch"), P(None, "ch"), P("seq", "ch"), P("seq", "ch"))
    return jax.shard_map(
        local,
        mesh=mesh,
        in_specs=placed,
        out_specs=(P("seq", "ch"),) * 4,
        check_vma=False,
    )
```

```python
import functools
import math

import jax
import jax.numpy as jnp
import ml_dtypes
import numpy as np
from jax import lax
from jax.experimental import pallas as pl
from jax.experimental.pallas import tpu as pltpu
from jax.sharding import PartitionSpec as P

MESH = pl.DeviceIdType.MESH
F32 = jnp.float32
BF16 = jnp.bfloat16
SIDE = 128
PADDED = SIDE * SIDE
SEQ = PADDED // 2
SCALE = SEQ**-0.5
ORDER = (4, 3, 5, 2, 6, 1, 7)


def split(table):
    high = table.astype(ml_dtypes.bfloat16)
    low = (table - high.astype(np.float64)).astype(ml_dtypes.bfloat16)
    return high, low


def tables():
    half = np.arange(64) + 0.5
    block = 2 * math.pi * np.outer(half, np.arange(64)) / SIDE
    first = np.concatenate([np.cos(block), -np.sin(block)], axis=0)
    first = np.concatenate(split(first), axis=1)
    twist = 2 * math.pi * np.outer(half, np.arange(SIDE)) / PADDED
    twist = np.concatenate([np.cos(twist), np.sin(twist)], axis=0).astype(np.float32)
    inner = 2 * math.pi * np.outer(np.arange(SIDE), np.arange(SIDE)) / SIDE
    c, s = np.cos(inner), np.sin(inner)
    forward = np.block([[c, -s], [s, c]])
    inverse = np.block([[c, s], [-s, c]])
    second = np.concatenate(split(forward) + split(inverse), axis=0)
    last = np.concatenate([np.cos(block.T), -np.sin(block.T)], axis=1) * (2.0 / PADDED)
    high, low = split(last)
    last = np.concatenate([high, high, low], axis=1)
    return tuple(t.astype(np.float32) for t in (first, twist, second, last))


def dot(a, b):
    return jnp.dot(a, b, preferred_element_type=F32)


def halves(x):
    high = x.astype(BF16)
    return high, (x - high.astype(F32)).astype(BF16)


def kernel(
    tok_in, vw_in, gw_in, fil_in, cot_in, t_first_in, t_twist_in, t_second_in, t_last_in,
    input_grad, filter_grad, vw_grad, gw_grad,
    tok, vw, gw, fil, cot, t_first, t_twist, t_second, t_last,
    t_first16, t_second16, t_last16, s_e, s_l, r1_e, r1_l, r2_e, r2_l, u_e, u_l, w_vg, w_f,
    spec, lhs, mid, s3, r3, r3s, r4, s3f, r3f, s4f, r4f,
    tk, g_all, part, r5, s6, r6, vt, gt, s7, r7, s8, r8,
    sem_qe, sem_ql, sem_ze, sem_zl, sem_zv, sem_zf, sem_qv, sem_qf, sem_q6,
    sem_tk, sem_sib, sem_rs, sem_c7, sem_x8, sem_own, sem_in,
):
    i = lax.axis_index("seq")
    c = lax.axis_index("ch")
    z, q = i // 8, i % 8
    core, xh = c % 2, c // 2
    sib = c + 1 - 2 * core
    opp = (c + 2) % 4

    def along_z(zz):
        return (zz * 8 + q, c)

    def along_q(qq):
        return (z * 8 + qq, c)

    loads = {}
    for at, (name, src, dst) in enumerate(
        (
            ("fil", fil_in, fil),
            ("cot", cot_in, cot),
            ("tok", tok_in, tok),
            ("vw", vw_in, vw),
            ("gw", gw_in, gw),
            ("first", t_first_in, t_first),
            ("twist", t_twist_in, t_twist),
            ("second", t_second_in, t_second),
            ("last", t_last_in, t_last),
        )
    ):
        loads[name] = pltpu.make_async_copy(src, dst, sem_in.at[at])
        loads[name].start()

    barrier = pltpu.get_barrier_semaphore()
    peers = 0
    for d in range(1, 8):
        for who in (along_z((z + d) % 8), along_q((q + d) % 8), (((z + d) % 8) * 8 + q, sib)):
            pl.semaphore_signal(barrier, inc=1, device_id=who, device_id_type=MESH)
            peers += 1
    for who in ((i, sib), (i, opp)):
        pl.semaphore_signal(barrier, inc=1, device_id=who, device_id_type=MESH)
        peers += 1

    def pair(a, b):
        a = a.T.reshape(16, 8, SIDE)
        b = b.T.reshape(16, 8, SIDE)
        return jnp.concatenate([a, b], axis=1).astype(BF16).reshape(2, SIDE, SIDE)

    pending = []

    def send(src, dst, ssem, rsem, who):
        copy = pltpu.make_async_remote_copy(
            src_ref=src, dst_ref=dst, send_sem=ssem, recv_sem=rsem, device_id=who, device_id_type=MESH
        )
        copy.start()
        pending.append(copy)

    def arrived(dst, sem, who):
        pltpu.make_async_remote_copy(
            src_ref=dst, dst_ref=dst, send_sem=sem.at[0, 0], recv_sem=sem.at[1, who],
            device_id=(i, sib), device_id_type=MESH,
        ).wait_recv()

    def exchange(me, reach, source, landing, sem):
        for d in ORDER:
            peer = (me + d) % 8
            send(source(peer), landing(me), sem.at[0, d], sem.at[1, me], reach(peer))

    def collect(me, landing, sem):
        for d in ORDER:
            peer = (me + d) % 8
            arrived(landing(peer), sem, peer)

    def rows16(ref, at):
        return ref.at[:, pl.ds(pl.multiple_of(at * 16, 16), 16), :]

    loads["fil"].wait()
    loads["cot"].wait()
    for b in range(4):
        lanes = slice(b * SIDE, (b + 1) * SIDE)
        s_e[2 * b : 2 * b + 2] = pair(fil[:, lanes], cot[:, lanes].astype(F32))
    loads["tok"].wait()
    own_cols = pl.ds(pl.multiple_of(core * 1024, 1024), 1024)
    own = pltpu.make_async_copy(tok.at[:, own_cols], tk.at[q], sem_own)
    own.start()

    pl.semaphore_wait(barrier, peers)
    exchange(q, along_q, lambda p: s_e.at[p], lambda p: r1_e.at[p], sem_qe)
    r1_e[pl.ds(q, 1)] = s_e[pl.ds(q, 1)]

    loads["vw"].wait()
    loads["gw"].wait()
    for b in range(2):
        lanes = slice(b * 256, (b + 1) * 256)
        val = dot(tok[...], vw[:, lanes])
        up = dot(tok[...], gw[:, lanes]) * cot[:, lanes].astype(F32)
        for e in range(2):
            part_lanes = slice(e * SIDE, (e + 1) * SIDE)
            at = 4 * b + 2 * e
            s_l[at : at + 2] = pair(val[:, part_lanes], up[:, part_lanes])
    exchange(q, along_q, lambda p: s_l.at[p], lambda p: r1_l.at[p], sem_ql)
    r1_l[pl.ds(q, 1)] = s_l[pl.ds(q, 1)]

    def second_phase(r1, r2, sem_q, sem_z):
        collect(q, lambda p: r1.at[p], sem_q)
        exchange(z, along_z, lambda p: rows16(r1, p), lambda p: r2.at[p], sem_z)
        mine = r1[:, pl.ds(pl.multiple_of(z * 16, 16), 16), :]
        r2[pl.ds(z, 1)] = mine.reshape(1, 8, 16, SIDE)

    for name in ("first", "twist", "second", "last"):
        loads[name].wait()
    cw = t_twist[0:64]
    sw = t_twist[64:128]
    for t in range(4):
        t_second16[t] = t_second[256 * t : 256 * (t + 1)].astype(BF16)
    t_first16[...] = t_first[...].astype(BF16)
    t_last16[...] = t_last[...].astype(BF16)
    g_high, g_low, i_high, i_low = (t_second16[t] for t in range(4))

    second_phase(r1_e, r2_e, sem_qe, sem_ze)
    for d in ORDER:
        peer = (q + d) % 8
        send(tok.at[:, own_cols], tk.at[q], sem_tk.at[0, d], sem_tk.at[1, q], along_q(peer))
    second_phase(r1_l, r2_l, sem_ql, sem_zl)

    def put(at, x):
        high, low = halves(x)
        lhs[0, at * 64 : (at + 1) * 64] = high
        lhs[1, at * 64 : (at + 1) * 64] = low

    def widen(r2, u):
        for zz in range(8):
            u[zz * SIDE : (zz + 1) * SIDE] = r2[zz].reshape(SIDE, SIDE).astype(F32)

    def forward(u, base, out):
        for r in range(0, 8, 2):
            x = [u[pl.ds(base + r + e, 64, stride=16), :] for e in range(2)]
            x = jnp.concatenate(x, axis=1).astype(BF16)
            a = dot(t_first16[...], jnp.concatenate([x, x], axis=0))
            for e in range(2):
                re = a[:64, e * SIDE : (e + 1) * SIDE]
                im = a[64:, e * SIDE : (e + 1) * SIDE]
                put(r + e, jnp.concatenate([re * cw + im * sw, im * cw - re * sw], axis=1))
        spec[out] = dot(lhs[0], g_high) + (dot(lhs[1], g_high) + dot(lhs[0], g_low))

    def inverse(left, right, conjugate, store):
        for r in range(8):
            rows = slice(r * 64, (r + 1) * 64)
            ar, ai = spec[left, rows, :SIDE], spec[left, rows, SIDE:]
            br, bi = spec[right, rows, :SIDE], spec[right, rows, SIDE:]
            if conjugate:
                p = [ar * br + ai * bi, ar * bi - ai * br]
            else:
                p = [ar * br - ai * bi, ar * bi + ai * br]
            put(r, jnp.concatenate(p, axis=1))
        mid[...] = dot(lhs[0], i_high) + (dot(lhs[1], i_high) + dot(lhs[0], i_low))
        for r in range(0, 8, 2):
            cols = []
            for e in range(2):
                rows = slice((r + e) * 64, (r + e + 1) * 64)
                re, im = mid[rows, :SIDE], mid[rows, SIDE:]
                cols.append(jnp.concatenate([re * cw - im * sw, im * cw + re * sw], axis=0))
            high, low = halves(jnp.concatenate(cols, axis=1))
            y = dot(t_last16[...], jnp.concatenate([high, low, high], axis=0))
            for e in range(2):
                store(r + e, y[:, e * SIDE : (e + 1) * SIDE])

    collect(z, lambda p: r2_e.at[p], sem_ze)
    widen(r2_e, u_e)
    forward(u_e, 0, 0)
    collect(z, lambda p: r2_l.at[p], sem_zl)
    widen(r2_l, u_l)
    forward(u_l, 8, 2)
    forward(u_l, 0, 1)

    def store_v(r, y):
        w_vg[pl.ds(r, 64, stride=16), :] = y

    def store_g(r, y):
        w_vg[pl.ds(8 + r, 64, stride=16), :] = y * u_e[pl.ds(8 + r, 64, stride=16), :]

    def store_f(r, y):
        w_f[pl.ds(r, 64, stride=8), :] = y

    inverse(0, 2, True, store_v)
    inverse(0, 1, False, store_g)
    for zz in range(8):
        s3[zz] = w_vg[zz * SIDE : (zz + 1) * SIDE].astype(BF16)
    exchange(z, along_z, lambda p: s3.at[p], lambda p: r3.at[p], sem_zv)
    r3[pl.ds(z, 1)] = s3[pl.ds(z, 1)]
    inverse(1, 2, True, store_f)
    for zz in range(8):
        s3f[zz] = w_f[zz * 64 : (zz + 1) * 64].astype(BF16)
    exchange(z, along_z, lambda p: s3f.at[p], lambda p: r3f.at[p], sem_zf)
    r3f[pl.ds(z, 1)] = s3f[pl.ds(z, 1)]

    send(r3.at[z], r3s.at[z], sem_sib.at[0, 0], sem_sib.at[1, z], (i, sib))
    for d in ORDER:
        peer = (z + d) % 8
        arrived(r3.at[peer], sem_zv, peer)
        send(r3.at[peer], r3s.at[peer], sem_sib.at[0, d], sem_sib.at[1, peer], (i, sib))
    exchange(q, along_q, lambda p: rows16(r3, p), lambda p: r4.at[p], sem_qv)
    r4[pl.ds(q, 1)] = r3[:, pl.ds(pl.multiple_of(q * 16, 16), 16), :].reshape(1, 8, 16, SIDE)

    collect(q, lambda p: tk.at[p], sem_tk)
    own.wait()
    for qq in range(8):
        g_all[0:SIDE, qq * SIDE : (qq + 1) * SIDE] = r3[:, qq * 16 : (qq + 1) * 16, :].reshape(SIDE, SIDE)
    for d in ORDER + (0,):
        arrived(r3s.at[(z + d) % 8], sem_sib, (z + d) % 8)
    for qq in range(8):
        g_all[SIDE:, qq * SIDE : (qq + 1) * SIDE] = r3s[:, qq * 16 : (qq + 1) * 16, :].reshape(SIDE, SIDE)
    for t in range(4):
        block = tk[:, :, t * 256 : (t + 1) * 256].reshape(1024, 256)
        sums = dot(g_all[...], block).astype(BF16)
        part[t, 0] = sums[:SIDE]
        part[t, 1] = sums[SIDE:]
        to = core * 4 + t

        def share(s, who, t=t, to=to):
            return pltpu.make_async_remote_copy(
                src_ref=part.at[t, s], dst_ref=r5.at[z], send_sem=sem_rs.at[0, 2 * t + s],
                recv_sem=sem_rs.at[1, z], device_id=(to * 8 + q, who), device_id_type=MESH,
            )

        share(1, sib).start()

        @pl.when(to != z)
        def _():
            share(0, c).start()

        @pl.when(to == z)
        def _():
            r5[pl.ds(z, 1)] = part[t, 0].reshape(1, SIDE, 256)

    collect(q, lambda p: r4.at[p], sem_qv)
    for qq in range(8):
        x = r4[qq].astype(F32)
        vt[:, qq * 64 : (qq + 1) * 64] = x[:, :8].reshape(64, SIDE).T.astype(BF16)
        gt[:, qq * 64 : (qq + 1) * 64] = x[:, 8:].reshape(64, SIDE).T.astype(BF16)

    def columns(k):
        rows = pl.ds(pl.multiple_of(k * 512, 512), 512)
        over = (((1,), (1,)), ((), ()))
        a = lax.dot_general(vt[...], vw[rows, :], over, preferred_element_type=F32)
        return a + lax.dot_general(gt[...], gw[rows, :], over, preferred_element_type=F32)

    s7[0] = columns(2 * (1 - xh) + 1 - core)
    s7[1] = columns(2 * xh + 1 - core)
    send(s7, r7, sem_c7.at[0, 0], sem_c7.at[1, 0], (i, sib))
    far = columns(2 * (1 - xh) + core)
    near = columns(2 * xh + core)
    arrived(r7, sem_c7, 0)
    s8[...] = (far + r7[0]).astype(BF16)
    send(s8, r8, sem_x8.at[0, 0], sem_x8.at[1, 0], (i, opp))
    near = near + r7[1]

    collect(z, lambda p: r3f.at[p], sem_zf)
    x = r3f[...].astype(F32).reshape(8, 8, 8, SIDE)
    for qq in range(8):
        s4f[qq] = x[:, qq].reshape(64, SIDE).astype(BF16)
    exchange(q, along_q, lambda p: s4f.at[p], lambda p: r4f.at[p], sem_qf)
    r4f[pl.ds(q, 1)] = s4f[pl.ds(q, 1)]

    for d in ORDER:
        peer = (z + d) % 8
        arrived(r5.at[peer], sem_rs, peer)

    @pl.when(core != z // 4)
    def _():
        arrived(r5.at[z], sem_rs, z)

    total = r5[0].astype(F32)
    for zz in range(1, 8):
        total = total + r5[zz].astype(F32)
    total = total.reshape(8, 2, 8, 256)
    total = jnp.concatenate([total[:, 0].reshape(64, 256), total[:, 1].reshape(64, 256)], axis=0)
    s6[...] = (total.T * SCALE).reshape(8, 32, SIDE)
    exchange(q, along_q, lambda p: s6.at[p], lambda p: r6.at[p], sem_q6)
    r6[pl.ds(q, 1)] = s6[pl.ds(q, 1)]

    arrived(r8, sem_x8, 0)
    input_grad[...] = (near + r8[...].astype(F32)).astype(BF16)

    collect(q, lambda p: r4f.at[p], sem_qf)
    for b in range(4):
        x = r4f[2 * b : 2 * b + 2].astype(F32).reshape(SIDE, SIDE)
        filter_grad[:, b * SIDE : (b + 1) * SIDE] = x.T * SCALE

    collect(q, lambda p: r6.at[p], sem_q6)
    for qq in range(8):
        vw_grad[:, qq * 64 : (qq + 1) * 64] = r6[qq, :, :64]
        gw_grad[:, qq * 64 : (qq + 1) * 64] = r6[qq, :, 64:]

    for copy in pending:
        copy.wait_send()
    for t in range(4):
        for s in range(2):
            copy = pltpu.make_async_remote_copy(
                src_ref=part.at[t, s], dst_ref=r5.at[z], send_sem=sem_rs.at[0, 2 * t + s],
                recv_sem=sem_rs.at[1, z], device_id=(i, sib), device_id_type=MESH,
            )
            if s == 1:
                copy.wait_send()
            else:

                @pl.when(core * 4 + t != z)
                def _(copy=copy):
                    copy.wait_send()


def local(tokens, value_weight, gate_weight, filters, cotangent):
    def v(*shape, dtype=BF16):
        return pltpu.VMEM(shape, dtype)

    sem = pltpu.SemaphoreType.DMA((2, 8))
    vmem = pl.BlockSpec(memory_space=pltpu.VMEM)
    whole = pl.BlockSpec(memory_space=pl.ANY)
    operands = [tokens, value_weight, gate_weight, filters, cotangent]
    operands += [jnp.asarray(t) for t in tables()]
    shape = jax.ShapeDtypeStruct
    results = pl.pallas_call(
        kernel,
        out_shape=(
            shape((128, 512), BF16),
            shape((128, 512), F32),
            shape((32, 512), F32),
            shape((32, 512), F32),
        ),
        in_specs=[whole] * 9,
        out_specs=(vmem,) * 4,
        scratch_shapes=[pltpu.VMEM(t.shape, t.dtype) for t in operands] + [
            v(128, 128), v(4, 256, 256), v(64, 384),
            v(8, 128, 128), v(8, 128, 128), v(8, 128, 128), v(8, 128, 128),
            v(8, 8, 16, 128), v(8, 8, 16, 128),
            v(1024, 128, dtype=F32), v(1024, 128, dtype=F32), v(1024, 128, dtype=F32), v(512, 128, dtype=F32),
            v(3, 512, 256, dtype=F32), v(2, 512, 256), v(512, 256, dtype=F32),
            v(8, 128, 128), v(8, 128, 128), v(8, 128, 128), v(8, 8, 16, 128),
            v(8, 64, 128), v(8, 64, 128), v(8, 64, 128), v(8, 64, 128),
            v(8, 128, 1024), v(256, 1024), v(4, 2, 128, 256), v(8, 128, 256),
            v(8, 32, 128, dtype=F32), v(8, 32, 128, dtype=F32),
            v(128, 512), v(128, 512),
            v(2, 128, 512, dtype=F32), v(2, 128, 512, dtype=F32), v(128, 512), v(128, 512),
        ] + [sem] * 14 + [pltpu.SemaphoreType.DMA, pltpu.SemaphoreType.DMA((9,))],
        compiler_params=pltpu.CompilerParams(
            collective_id=0, has_side_effects=True, vmem_limit_bytes=60 * 1024 * 1024
        ),
        cost_estimate=pl.CostEstimate(flops=3_000_000_000, bytes_accessed=8_000_000, transcendentals=0),
    )(*operands)
    return pl.pallas_call(
        hand_over,
        out_shape=tuple(shape(r.shape, r.dtype) for r in results),
        in_specs=[whole] * 4,
        out_specs=(whole,) * 4,
        scratch_shapes=[pltpu.SemaphoreType.DMA((4,))],
        compiler_params=pltpu.CompilerParams(vmem_limit_bytes=60 * 1024 * 1024),
    )(*results)


def hand_over(*refs):
    copies = [pltpu.make_async_copy(refs[t], refs[4 + t], refs[8].at[t]) for t in range(4)]
    for copy in copies:
        copy.start()
    for copy in copies:
        copy.wait()


def solution(mesh):
    placed = (P("seq", None), P(None, "ch"), P(None, "ch"), P("seq", "ch"), P("seq", "ch"))
    return jax.shard_map(
        local,
        mesh=mesh,
        in_specs=placed,
        out_specs=(P("seq", "ch"),) * 4,
        check_vma=False,
    )
```

```python
import functools
import math

import jax
import jax.numpy as jnp
import ml_dtypes
import numpy as np
from jax import lax
from jax.experimental import pallas as pl
from jax.experimental.pallas import tpu as pltpu
from jax.sharding import PartitionSpec as P

MESH = pl.DeviceIdType.MESH
F32 = jnp.float32
BF16 = jnp.bfloat16
SIDE = 128
PADDED = SIDE * SIDE
SEQ = PADDED // 2
SCALE = SEQ**-0.5
ORDER = (4, 3, 5, 2, 6, 1, 7)
NEAR = ((0, 0), (1, 0), (0, 1), (0, 3), (1, 1), (1, 3), (0, 2), (1, 2))
BACK = (0, 1, 3, 2, 5, 4, 6, 7)
GROUPS = ((0, 1), (1, 4), (4, 8))


def split(table):
    high = table.astype(ml_dtypes.bfloat16)
    low = (table - high.astype(np.float64)).astype(ml_dtypes.bfloat16)
    return high, low


def tables():
    half = np.arange(64) + 0.5
    block = 2 * math.pi * np.outer(half, np.arange(64)) / SIDE
    first = np.concatenate([np.cos(block), -np.sin(block)], axis=0)
    first = np.concatenate(split(first), axis=1)
    twist = 2 * math.pi * np.outer(half, np.arange(SIDE)) / PADDED
    twist = np.concatenate([np.cos(twist), np.sin(twist)], axis=0).astype(np.float32)
    inner = 2 * math.pi * np.outer(np.arange(SIDE), np.arange(SIDE)) / SIDE
    c, s = np.cos(inner), np.sin(inner)
    forward = np.block([[c, -s], [s, c]])
    inverse = np.block([[c, s], [-s, c]])
    second = np.concatenate(split(forward) + split(inverse), axis=0)
    last = np.concatenate([np.cos(block.T), -np.sin(block.T)], axis=1) * (2.0 / PADDED)
    high, low = split(last)
    last = np.concatenate([high, high, low], axis=1)
    return tuple(t.astype(np.float32) for t in (first, twist, second, last))


def dot(a, b):
    return jnp.dot(a, b, preferred_element_type=F32)


def halves(x):
    high = x.astype(BF16)
    return high, (x - high.astype(F32)).astype(BF16)


def kernel(
    tok_in, vw_in, gw_in, fil_in, cot_in, t_first_in, t_twist_in, t_second_in, t_last_in,
    input_grad, filter_grad, vw_grad, gw_grad,
    tok, vw, gw, fil, cot, t_first, t_twist, t_second, t_last,
    t_first16, t_second16, t_last16, s_e, s_l, r1_e, r1_l, r2_e, r2_l, u_e, u_l, w_vg, w_f,
    spec, lhs, mid, s3, r3, r3s, r4, s3f, r3f, s4f, r4f,
    tk, g_all, part, r5, s6, r6, vt, gt, s7, r7, s8, r8,
    sem_qe, sem_ql, sem_ze, sem_zl, sem_zv, sem_zf, sem_qv, sem_qf, sem_q6,
    sem_tk, sem_sib, sem_rs, sem_c7, sem_x8, sem_own, sem_in,
):
    i = lax.axis_index("seq")
    c = lax.axis_index("ch")
    z, q = i // 8, i % 8
    core, xh = c % 2, c // 2
    sib = c + 1 - 2 * core
    opp = (c + 2) % 4

    def along_z(zz):
        return (zz * 8 + q, c)

    def along_q(qq):
        return (z * 8 + qq, c)

    def near(slot):
        dx, dy = NEAR[slot]
        return (q // 4 + dx) % 2 * 4 + (q + dy) % 4

    loads = {}
    for at, (name, src, dst) in enumerate(
        (
            ("fil", fil_in, fil),
            ("cot", cot_in, cot),
            ("tok", tok_in, tok),
            ("vw", vw_in, vw),
            ("gw", gw_in, gw),
            ("first", t_first_in, t_first),
            ("twist", t_twist_in, t_twist),
            ("second", t_second_in, t_second),
            ("last", t_last_in, t_last),
        )
    ):
        loads[name] = pltpu.make_async_copy(src, dst, sem_in.at[at])
        loads[name].start()

    barrier = pltpu.get_barrier_semaphore()
    peers = 0
    for d in range(1, 8):
        for who in (along_z((z + d) % 8), along_q((q + d) % 8), (((z + d) % 8) * 8 + q, sib)):
            pl.semaphore_signal(barrier, inc=1, device_id=who, device_id_type=MESH)
            peers += 1
    for who in ((i, sib), (i, opp)):
        pl.semaphore_signal(barrier, inc=1, device_id=who, device_id_type=MESH)
        peers += 1

    def pair(a, b):
        a = a.T.reshape(16, 8, SIDE)
        b = b.T.reshape(16, 8, SIDE)
        return jnp.concatenate([a, b], axis=1).astype(BF16).reshape(2, SIDE, SIDE)

    pending = []

    def send(src, dst, ssem, rsem, who):
        copy = pltpu.make_async_remote_copy(
            src_ref=src, dst_ref=dst, send_sem=ssem, recv_sem=rsem, device_id=who, device_id_type=MESH
        )
        copy.start()
        pending.append(copy)

    def arrived(dst, sem, who):
        pltpu.make_async_remote_copy(
            src_ref=dst, dst_ref=dst, send_sem=sem.at[0, 0], recv_sem=sem.at[1, who],
            device_id=(i, sib), device_id_type=MESH,
        ).wait_recv()

    def exchange(me, reach, source, landing, sem):
        for d in ORDER:
            peer = (me + d) % 8
            send(source(peer), landing(me), sem.at[0, d], sem.at[1, me], reach(peer))

    def collect(me, landing, sem):
        for d in ORDER:
            peer = (me + d) % 8
            arrived(landing(peer), sem, peer)

    def rows16(ref, at):
        return ref.at[:, pl.ds(pl.multiple_of(at * 16, 16), 16), :]

    loads["fil"].wait()
    loads["cot"].wait()
    for b in range(4):
        lanes = slice(b * SIDE, (b + 1) * SIDE)
        s_e[2 * b : 2 * b + 2] = pair(fil[:, lanes], cot[:, lanes].astype(F32))
    loads["tok"].wait()
    own_cols = pl.ds(pl.multiple_of(core * 1024, 1024), 1024)
    own = pltpu.make_async_copy(tok.at[:, own_cols], tk.at[q], sem_own)
    own.start()

    pl.semaphore_wait(barrier, peers)
    exchange(z, along_z, lambda p: rows16(s_e, p), lambda p: r1_e.at[p], sem_ze)
    r1_e[pl.ds(z, 1)] = s_e[:, pl.ds(pl.multiple_of(z * 16, 16), 16), :].reshape(1, 8, 16, SIDE)

    def give(src, dst, at, slot):
        send(src, dst, sem_tk.at[0, at], sem_tk.at[1, at], along_q(near(slot)))

    half = tok.at[:, own_cols]
    for at, slot in ((0, 1), (1, 3), (2, 2)):
        give(half, tk.at[q], at, slot)

    loads["vw"].wait()
    loads["gw"].wait()
    for b in range(2):
        lanes = slice(b * 256, (b + 1) * 256)
        val = dot(tok[...], vw[:, lanes])
        up = dot(tok[...], gw[:, lanes]) * cot[:, lanes].astype(F32)
        for e in range(2):
            part_lanes = slice(e * SIDE, (e + 1) * SIDE)
            at = 4 * b + 2 * e
            s_l[at : at + 2] = pair(val[:, part_lanes], up[:, part_lanes])
    for slot in range(1, 8):
        send(
            s_l.at[near(slot)], r1_l.at[BACK[slot]],
            sem_ql.at[0, slot], sem_ql.at[1, BACK[slot]], along_q(near(slot)),
        )
    r1_l[0] = s_l[pl.ds(q, 1)].reshape(SIDE, SIDE)

    def onward(group):
        a, b = GROUPS[group]
        for slot in range(max(a, 1), b):
            arrived(r1_l.at[slot], sem_ql, slot)
        for d in ORDER:
            peer = (z + d) % 8
            rows = pl.ds(pl.multiple_of(peer * 16, 16), 16)
            send(
                r1_l.at[a:b, rows, :], r2_l.at[z, a:b],
                sem_zl.at[0, 8 * group + d], sem_zl.at[1, 8 * group + z], along_z(peer),
            )
        mine = r1_l[a:b, pl.ds(pl.multiple_of(z * 16, 16), 16), :]
        r2_l[pl.ds(z, 1), a:b] = mine.reshape(1, b - a, 16, SIDE)

    onward(0)
    for name in ("first", "twist", "second", "last"):
        loads[name].wait()
    cw = t_twist[0:64]
    sw = t_twist[64:128]
    for t in range(4):
        t_second16[t] = t_second[256 * t : 256 * (t + 1)].astype(BF16)
    t_first16[...] = t_first[...].astype(BF16)
    t_last16[...] = t_last[...].astype(BF16)
    g_high, g_low, i_high, i_low = (t_second16[t] for t in range(4))

    collect(z, lambda p: r1_e.at[p], sem_ze)
    exchange(q, along_q, lambda p: r1_e.at[:, p], lambda p: r2_e.at[:, p], sem_qe)
    r2_e[:, pl.ds(q, 1)] = r1_e[:, pl.ds(q, 1)]
    onward(1)
    onward(2)
    arrived(tk.at[near(1)], sem_tk, 0)
    give(tk.at[near(1)], tk.at[near(1)], 3, 3)
    give(tk.at[near(1)], tk.at[near(1)], 4, 2)

    def put(at, x):
        high, low = halves(x)
        lhs[0, at * 64 : (at + 1) * 64] = high
        lhs[1, at * 64 : (at + 1) * 64] = low

    def forward(u, base, out):
        for r in range(0, 8, 2):
            x = [u[pl.ds(base + r + e, 64, stride=16), :] for e in range(2)]
            x = jnp.concatenate(x, axis=1).astype(BF16)
            a = dot(t_first16[...], jnp.concatenate([x, x], axis=0))
            for e in range(2):
                re = a[:64, e * SIDE : (e + 1) * SIDE]
                im = a[64:, e * SIDE : (e + 1) * SIDE]
                put(r + e, jnp.concatenate([re * cw + im * sw, im * cw - re * sw], axis=1))
        spec[out] = dot(lhs[0], g_high) + (dot(lhs[1], g_high) + dot(lhs[0], g_low))

    def inverse(left, right, conjugate, store):
        for r in range(8):
            rows = slice(r * 64, (r + 1) * 64)
            ar, ai = spec[left, rows, :SIDE], spec[left, rows, SIDE:]
            br, bi = spec[right, rows, :SIDE], spec[right, rows, SIDE:]
            if conjugate:
                p = [ar * br + ai * bi, ar * bi - ai * br]
            else:
                p = [ar * br - ai * bi, ar * bi + ai * br]
            put(r, jnp.concatenate(p, axis=1))
        mid[...] = dot(lhs[0], i_high) + (dot(lhs[1], i_high) + dot(lhs[0], i_low))
        for r in range(0, 8, 2):
            cols = []
            for e in range(2):
                rows = slice((r + e) * 64, (r + e + 1) * 64)
                re, im = mid[rows, :SIDE], mid[rows, SIDE:]
                cols.append(jnp.concatenate([re * cw - im * sw, im * cw + re * sw], axis=0))
            high, low = halves(jnp.concatenate(cols, axis=1))
            y = dot(t_last16[...], jnp.concatenate([high, low, high], axis=0))
            for e in range(2):
                store(r + e, y[:, e * SIDE : (e + 1) * SIDE])

    collect(q, lambda p: r2_e.at[:, p], sem_qe)
    for zz in range(8):
        u_e[zz * SIDE : (zz + 1) * SIDE] = r2_e[zz].reshape(SIDE, SIDE).astype(F32)
    forward(u_e, 0, 0)
    for group, (a, b) in enumerate(GROUPS):
        for d in ORDER:
            peer = (z + d) % 8
            arrived(r2_l.at[peer, a:b], sem_zl, 8 * group + peer)
        for slot in range(a, b):
            for zz in range(8):
                at = pl.multiple_of(zz * SIDE + near(slot) * 16, 16)
                u_l[pl.ds(at, 16), :] = r2_l[zz, slot].astype(F32)
    forward(u_l, 8, 2)
    forward(u_l, 0, 1)

    def store_v(r, y):
        w_vg[pl.ds(r, 64, stride=16), :] = y

    def store_g(r, y):
        w_vg[pl.ds(8 + r, 64, stride=16), :] = y * u_e[pl.ds(8 + r, 64, stride=16), :]

    def store_f(r, y):
        w_f[pl.ds(r, 64, stride=8), :] = y

    inverse(0, 2, True, store_v)
    inverse(0, 1, False, store_g)
    for zz in range(8):
        s3[zz] = w_vg[zz * SIDE : (zz + 1) * SIDE].astype(BF16)
    exchange(z, along_z, lambda p: s3.at[p], lambda p: r3.at[p], sem_zv)
    r3[pl.ds(z, 1)] = s3[pl.ds(z, 1)]
    inverse(1, 2, True, store_f)
    for zz in range(8):
        s3f[zz] = w_f[zz * 64 : (zz + 1) * 64].astype(BF16)
    exchange(z, along_z, lambda p: s3f.at[p], lambda p: r3f.at[p], sem_zf)
    r3f[pl.ds(z, 1)] = s3f[pl.ds(z, 1)]

    for at, slot in ((1, 2), (2, 3), (3, 4), (4, 5)):
        arrived(tk.at[near(slot)], sem_tk, at)
    for at, slot in ((5, 2), (6, 4)):
        give(tk.at[near(slot), 0:64], tk.at[near(slot), 0:64], at, 3)
    for at, slot in ((7, 3), (8, 5)):
        give(tk.at[near(slot), 64:SIDE], tk.at[near(slot), 64:SIDE], at, 2)

    send(r3.at[z], r3s.at[z], sem_sib.at[0, 0], sem_sib.at[1, z], (i, sib))
    for d in ORDER:
        peer = (z + d) % 8
        arrived(r3.at[peer], sem_zv, peer)
        send(r3.at[peer], r3s.at[peer], sem_sib.at[0, d], sem_sib.at[1, peer], (i, sib))
    exchange(q, along_q, lambda p: rows16(r3, p), lambda p: r4.at[p], sem_qv)
    r4[pl.ds(q, 1)] = r3[:, pl.ds(pl.multiple_of(q * 16, 16), 16), :].reshape(1, 8, 16, SIDE)

    for at, slot in ((5, 6), (6, 7)):
        arrived(tk.at[near(slot), 0:64], sem_tk, at)
        arrived(tk.at[near(slot), 64:SIDE], sem_tk, at + 2)
    own.wait()
    for qq in range(8):
        g_all[0:SIDE, qq * SIDE : (qq + 1) * SIDE] = r3[:, qq * 16 : (qq + 1) * 16, :].reshape(SIDE, SIDE)
    for d in ORDER + (0,):
        arrived(r3s.at[(z + d) % 8], sem_sib, (z + d) % 8)
    for qq in range(8):
        g_all[SIDE:, qq * SIDE : (qq + 1) * SIDE] = r3s[:, qq * 16 : (qq + 1) * 16, :].reshape(SIDE, SIDE)
    for t in range(4):
        block = tk[:, :, t * 256 : (t + 1) * 256].reshape(1024, 256)
        sums = dot(g_all[...], block).astype(BF16)
        part[t, 0] = sums[:SIDE]
        part[t, 1] = sums[SIDE:]
        to = core * 4 + t

        def share(s, who, t=t, to=to):
            return pltpu.make_async_remote_copy(
                src_ref=part.at[t, s], dst_ref=r5.at[z], send_sem=sem_rs.at[0, 2 * t + s],
                recv_sem=sem_rs.at[1, z], device_id=(to * 8 + q, who), device_id_type=MESH,
            )

        share(1, sib).start()

        @pl.when(to != z)
        def _():
            share(0, c).start()

        @pl.when(to == z)
        def _():
            r5[pl.ds(z, 1)] = part[t, 0].reshape(1, SIDE, 256)

    collect(q, lambda p: r4.at[p], sem_qv)
    for qq in range(8):
        x = r4[qq].astype(F32)
        vt[:, qq * 64 : (qq + 1) * 64] = x[:, :8].reshape(64, SIDE).T.astype(BF16)
        gt[:, qq * 64 : (qq + 1) * 64] = x[:, 8:].reshape(64, SIDE).T.astype(BF16)

    def columns(k):
        rows = pl.ds(pl.multiple_of(k * 512, 512), 512)
        over = (((1,), (1,)), ((), ()))
        a = lax.dot_general(vt[...], vw[rows, :], over, preferred_element_type=F32)
        return a + lax.dot_general(gt[...], gw[rows, :], over, preferred_element_type=F32)

    s7[0] = columns(2 * (1 - xh) + 1 - core)
    s7[1] = columns(2 * xh + 1 - core)
    send(s7, r7, sem_c7.at[0, 0], sem_c7.at[1, 0], (i, sib))
    far = columns(2 * (1 - xh) + core)
    here = columns(2 * xh + core)
    arrived(r7, sem_c7, 0)
    s8[...] = (far + r7[0]).astype(BF16)
    send(s8, r8, sem_x8.at[0, 0], sem_x8.at[1, 0], (i, opp))
    here = here + r7[1]

    collect(z, lambda p: r3f.at[p], sem_zf)
    x = r3f[...].astype(F32).reshape(8, 8, 8, SIDE)
    for qq in range(8):
        s4f[qq] = x[:, qq].reshape(64, SIDE).astype(BF16)
    exchange(q, along_q, lambda p: s4f.at[p], lambda p: r4f.at[p], sem_qf)
    r4f[pl.ds(q, 1)] = s4f[pl.ds(q, 1)]

    for d in ORDER:
        peer = (z + d) % 8
        arrived(r5.at[peer], sem_rs, peer)

    @pl.when(core != z // 4)
    def _():
        arrived(r5.at[z], sem_rs, z)

    total = r5[0].astype(F32)
    for zz in range(1, 8):
        total = total + r5[zz].astype(F32)
    total = total.reshape(8, 2, 8, 256)
    total = jnp.concatenate([total[:, 0].reshape(64, 256), total[:, 1].reshape(64, 256)], axis=0)
    s6[...] = (total.T * SCALE).reshape(8, 32, SIDE)
    exchange(q, along_q, lambda p: s6.at[p], lambda p: r6.at[p], sem_q6)
    r6[pl.ds(q, 1)] = s6[pl.ds(q, 1)]

    arrived(r8, sem_x8, 0)
    input_grad[...] = (here + r8[...].astype(F32)).astype(BF16)

    collect(q, lambda p: r4f.at[p], sem_qf)
    for b in range(4):
        x = r4f[2 * b : 2 * b + 2].astype(F32).reshape(SIDE, SIDE)
        filter_grad[:, b * SIDE : (b + 1) * SIDE] = x.T * SCALE

    collect(q, lambda p: r6.at[p], sem_q6)
    for qq in range(8):
        vw_grad[:, qq * 64 : (qq + 1) * 64] = r6[qq, :, :64]
        gw_grad[:, qq * 64 : (qq + 1) * 64] = r6[qq, :, 64:]

    for copy in pending:
        copy.wait_send()
    for t in range(4):
        for s in range(2):
            copy = pltpu.make_async_remote_copy(
                src_ref=part.at[t, s], dst_ref=r5.at[z], send_sem=sem_rs.at[0, 2 * t + s],
                recv_sem=sem_rs.at[1, z], device_id=(i, sib), device_id_type=MESH,
            )
            if s == 1:
                copy.wait_send()
            else:

                @pl.when(core * 4 + t != z)
                def _(copy=copy):
                    copy.wait_send()


def local(tokens, value_weight, gate_weight, filters, cotangent):
    def v(*shape, dtype=BF16):
        return pltpu.VMEM(shape, dtype)

    sem = pltpu.SemaphoreType.DMA((2, 24))
    vmem = pl.BlockSpec(memory_space=pltpu.VMEM)
    whole = pl.BlockSpec(memory_space=pl.ANY)
    operands = [tokens, value_weight, gate_weight, filters, cotangent]
    operands += [jnp.asarray(t) for t in tables()]
    shape = jax.ShapeDtypeStruct
    results = pl.pallas_call(
        kernel,
        out_shape=(
            shape((128, 512), BF16),
            shape((128, 512), F32),
            shape((32, 512), F32),
            shape((32, 512), F32),
        ),
        in_specs=[whole] * 9,
        out_specs=(vmem,) * 4,
        scratch_shapes=[pltpu.VMEM(t.shape, t.dtype) for t in operands] + [
            v(128, 128), v(4, 256, 256), v(64, 384),
            v(8, 128, 128), v(8, 128, 128), v(8, 8, 16, 128), v(8, 128, 128),
            v(8, 8, 16, 128), v(8, 8, 16, 128),
            v(1024, 128, dtype=F32), v(1024, 128, dtype=F32), v(1024, 128, dtype=F32), v(512, 128, dtype=F32),
            v(3, 512, 256, dtype=F32), v(2, 512, 256), v(512, 256, dtype=F32),
            v(8, 128, 128), v(8, 128, 128), v(8, 128, 128), v(8, 8, 16, 128),
            v(8, 64, 128), v(8, 64, 128), v(8, 64, 128), v(8, 64, 128),
            v(8, 128, 1024), v(256, 1024), v(4, 2, 128, 256), v(8, 128, 256),
            v(8, 32, 128, dtype=F32), v(8, 32, 128, dtype=F32),
            v(128, 512), v(128, 512),
            v(2, 128, 512, dtype=F32), v(2, 128, 512, dtype=F32), v(128, 512), v(128, 512),
        ] + [sem] * 14 + [pltpu.SemaphoreType.DMA, pltpu.SemaphoreType.DMA((9,))],
        compiler_params=pltpu.CompilerParams(
            collective_id=0, has_side_effects=True, vmem_limit_bytes=60 * 1024 * 1024
        ),
        cost_estimate=pl.CostEstimate(flops=3_000_000_000, bytes_accessed=8_000_000, transcendentals=0),
    )(*operands)
    return pl.pallas_call(
        hand_over,
        out_shape=tuple(shape(r.shape, r.dtype) for r in results),
        in_specs=[whole] * 4,
        out_specs=(whole,) * 4,
        scratch_shapes=[pltpu.VMEM(r.shape, r.dtype) for r in results] + [pltpu.SemaphoreType.DMA((8,))],
        compiler_params=pltpu.CompilerParams(vmem_limit_bytes=60 * 1024 * 1024),
    )(*results)


def hand_over(*refs):
    into = [pltpu.make_async_copy(refs[t], refs[8 + t], refs[12].at[t]) for t in range(4)]
    onto = [pltpu.make_async_copy(refs[8 + t], refs[4 + t], refs[12].at[4 + t]) for t in range(4)]
    for copy in into:
        copy.start()
    for copy, after in zip(into, onto):
        copy.wait()
        after.start()
    for copy in onto:
        copy.wait()


def solution(mesh):
    placed = (P("seq", None), P(None, "ch"), P(None, "ch"), P("seq", "ch"), P("seq", "ch"))
    return jax.shard_map(
        local,
        mesh=mesh,
        in_specs=placed,
        out_specs=(P("seq", "ch"),) * 4,
        check_vma=False,
    )
```

```python
import functools
import math

import jax
import jax.numpy as jnp
import ml_dtypes
import numpy as np
from jax import lax
from jax.experimental import pallas as pl
from jax.experimental.pallas import tpu as pltpu
from jax.sharding import PartitionSpec as P

MESH = pl.DeviceIdType.MESH
F32 = jnp.float32
BF16 = jnp.bfloat16
SIDE = 128
PADDED = SIDE * SIDE
SEQ = PADDED // 2
SCALE = SEQ**-0.5
ORDER = (4, 3, 5, 2, 6, 1, 7)
NEAR = ((0, 0), (1, 0), (0, 1), (0, 3), (1, 1), (1, 3), (0, 2), (1, 2))
BACK = (0, 1, 3, 2, 5, 4, 6, 7)
GROUPS = ((0, 1), (1, 4), (4, 8))
CLOSE, FAR = (2, 6, 1, 7), (4, 3, 5)
LOADS = ("fil", "cot", "tok", "vw", "gw", "first", "twist", "second", "last")
OUTGOING = ("ez", "eq", "lq", "lz", "cq", "vz", "sib", "fz", "vq", "fq", "tk", "rs", "core", "far")
INCOMING = (
    "ez", "eq", "lq1", "lq2", "lz0", "lz1", "lz2", "cq", "vzc", "vzf", "sibc", "sibf", "fz", "vq", "fq",
    "tk0", "tk1", "tk2", "rs", "core", "far",
)
SEMAPHORES = (
    tuple(t + ">" for t in OUTGOING)
    + tuple(">" + t for t in INCOMING)
    + ("own", "out0", "out1", "out2", "out3")
    + LOADS
)


def split(table):
    high = table.astype(ml_dtypes.bfloat16)
    low = (table - high.astype(np.float64)).astype(ml_dtypes.bfloat16)
    return high, low


def tables():
    half = np.arange(64) + 0.5
    block = 2 * math.pi * np.outer(half, np.arange(64)) / SIDE
    first = np.concatenate([np.cos(block), -np.sin(block)], axis=0)
    first = np.concatenate(split(first), axis=1)
    twist = 2 * math.pi * np.outer(half, np.arange(SIDE)) / PADDED
    twist = np.concatenate([np.cos(twist), np.sin(twist)], axis=0).astype(np.float32)
    inner = 2 * math.pi * np.outer(np.arange(SIDE), np.arange(SIDE)) / SIDE
    c, s = np.cos(inner), np.sin(inner)
    forward = np.block([[c, -s], [s, c]])
    inverse = np.block([[c, s], [-s, c]])
    second = np.concatenate(split(forward) + split(inverse), axis=0)
    last = np.concatenate([np.cos(block.T), -np.sin(block.T)], axis=1) * (2.0 / PADDED)
    high, low = split(last)
    last = np.concatenate([high, high, low], axis=1)
    return tuple(t.astype(np.float32) for t in (first, twist, second, last))


def dot(a, b):
    return jnp.dot(a, b, preferred_element_type=F32)


def halves(x):
    high = x.astype(BF16)
    return high, (x - high.astype(F32)).astype(BF16)


def kernel(
    tok_in, vw_in, gw_in, fil_in, cot_in, t_first_in, t_twist_in, t_second_in, t_last_in,
    input_grad, filter_grad, vw_grad, gw_grad,
    tok, vw, gw, fil, cot, t_first, t_twist, t_second, t_last,
    t_first16, t_second16, t_last16, s_e, s_l, r1_e, r1_l, s2_e, r2_e, r2_l, u_e, u_l, w_vg, w_f,
    s_c, r_c, wide_c,
    spec, lhs, mid, s3, r3, r3s, r4, s3f, r3f, s4f, r4f,
    tk, g_all, part, r5, vt, gt, s7, r7, s8, r8, o_in, o_fil, o_vw, o_gw, sems,
):
    i = lax.axis_index("seq")
    c = lax.axis_index("ch")
    z, q = i // 8, i % 8
    core, xh = c % 2, c // 2
    sib = c + 1 - 2 * core
    opp = (c + 2) % 4

    def along_z(zz):
        return (zz * 8 + q, c)

    def along_q(qq):
        return (z * 8 + qq, c)

    def near(slot):
        dx, dy = NEAR[slot]
        return (q // 4 + dx) % 2 * 4 + (q + dy) % 4

    def sem(name):
        return sems.at[SEMAPHORES.index(name)]

    loads = {}
    sources = (fil_in, cot_in, tok_in, vw_in, gw_in, t_first_in, t_twist_in, t_second_in, t_last_in)
    places = (fil, cot, tok, vw, gw, t_first, t_twist, t_second, t_last)
    for name, src, dst in zip(LOADS, sources, places):
        loads[name] = pltpu.make_async_copy(src, dst, sem(name))
        loads[name].start()

    barrier = pltpu.get_barrier_semaphore()
    peers = 0
    for d in range(1, 8):
        for who in (along_z((z + d) % 8), along_q((q + d) % 8)):
            pl.semaphore_signal(barrier, inc=1, device_id=who, device_id_type=MESH)
            peers += 1
    for who in ((i, sib), (i, opp), (along_q(near(1))[0], opp)):
        pl.semaphore_signal(barrier, inc=1, device_id=who, device_id_type=MESH)
        peers += 1

    def pair(a, b):
        a = a.T.reshape(16, 8, SIDE)
        b = b.T.reshape(16, 8, SIDE)
        return jnp.concatenate([a, b], axis=1).astype(BF16).reshape(2, SIDE, SIDE)

    def send(src, dst, out, into, who):
        pltpu.make_async_remote_copy(
            src_ref=src, dst_ref=dst, send_sem=sem(out), recv_sem=sem(into), device_id=who, device_id_type=MESH
        ).start()

    def waiter(size, out, into):
        return pltpu.make_async_remote_copy(
            src_ref=size, dst_ref=size, send_sem=sem(out), recv_sem=sem(into),
            device_id=(i, sib), device_id_type=MESH,
        )

    def arrived(size, out, into):
        waiter(size, out, into).wait_recv()

    def rows16(ref, at):
        return ref.at[:, pl.ds(pl.multiple_of(at * 16, 16), 16), :]

    loads["fil"].wait()
    for b in range(4):
        rows = fil[:, b * SIDE : (b + 1) * SIDE].T.reshape(2, 8, 8, SIDE)
        for zz in range(8):
            s_e[zz, b * 16 : (b + 1) * 16] = rows[:, zz].reshape(16, SIDE).astype(BF16)
    loads["tok"].wait()
    own_cols = pl.ds(pl.multiple_of(core * 1024, 1024), 1024)
    half = tok.at[:, own_cols]
    own = pltpu.make_async_copy(half, tk.at[q], sem("own"))
    own.start()

    pl.semaphore_wait(barrier, peers)
    for d in ORDER:
        peer = (z + d) % 8
        send(s_e.at[peer], r1_e.at[z], "ez>", ">ez", along_z(peer))
    r1_e[pl.ds(z, 1)] = s_e[pl.ds(z, 1)]

    loads["cot"].wait()
    loads["vw"].wait()
    loads["gw"].wait()
    for b in range(2):
        lanes = slice(b * 256, (b + 1) * 256)
        val = dot(tok[...], vw[:, lanes])
        up = dot(tok[...], gw[:, lanes]) * cot[:, lanes].astype(F32)
        for e in range(2):
            part_lanes = slice(e * SIDE, (e + 1) * SIDE)
            at = 4 * b + 2 * e
            s_l[at : at + 2] = pair(val[:, part_lanes], up[:, part_lanes])
    for group in (1, 2):
        for slot in range(*GROUPS[group]):
            send(s_l.at[near(slot)], r1_l.at[BACK[slot]], "lq>", f">lq{group}", along_q(near(slot)))
    r1_l[0] = s_l[pl.ds(q, 1)].reshape(SIDE, SIDE)

    def onward(group):
        a, b = GROUPS[group]
        if group:
            arrived(r1_l.at[a:b], "lq>", f">lq{group}")
        for d in ORDER:
            peer = (z + d) % 8
            rows = pl.ds(pl.multiple_of(peer * 16, 16), 16)
            send(r1_l.at[a:b, rows, :], r2_l.at[z, a:b], "lz>", f">lz{group}", along_z(peer))
        mine = r1_l[a:b, pl.ds(pl.multiple_of(z * 16, 16), 16), :]
        r2_l[pl.ds(z, 1), a:b] = mine.reshape(1, b - a, 16, SIDE)

    def give(src, dst, at, who):
        send(src, dst, "tk>", f">tk{at}", who)

    up_half, down_half = slice(0, 64), slice(64, SIDE)
    ahead, behind = along_q(near(2)), along_q(near(3))
    beside, across = along_q(near(1)), (along_q(near(1))[0], opp)

    def sideways(block):
        give(tk.at[block, up_half], tk.at[block, up_half], 2, beside)
        give(tk.at[block, down_half], tk.at[block, down_half], 2, across)

    onward(0)
    for name in ("first", "twist", "second", "last"):
        loads[name].wait()
    cw = t_twist[0:64]
    sw = t_twist[64:128]
    for t in range(4):
        t_second16[t] = t_second[256 * t : 256 * (t + 1)].astype(BF16)
    t_first16[...] = t_first[...].astype(BF16)
    t_last16[...] = t_last[...].astype(BF16)
    g_high, g_low, i_high, i_low = (t_second16[t] for t in range(4))
    for b in range(4):
        lanes = slice(b * SIDE, (b + 1) * SIDE)
        s_c[2 * b : 2 * b + 2] = cot[:, lanes].astype(F32).T.astype(BF16).reshape(2, 64, SIDE)
    onward(1)
    onward(2)

    def regroup(src, dst):
        x = src[...].astype(F32).reshape(8, 8, 8, SIDE)
        for qq in range(8):
            dst[qq] = x[:, qq].reshape(64, SIDE).astype(BF16)

    arrived(r1_e.at[0:7], "ez>", ">ez")
    regroup(r1_e, s2_e)
    for d in ORDER:
        peer = (q + d) % 8
        send(s2_e.at[peer], r2_e.at[q], "eq>", ">eq", along_q(peer))
    r2_e[pl.ds(q, 1)] = s2_e[pl.ds(q, 1)]
    give(half, tk.at[q], 0, ahead)
    give(half, tk.at[q], 0, behind)
    give(tok.at[up_half, own_cols], tk.at[q, up_half], 0, beside)
    give(tok.at[down_half, own_cols], tk.at[q, down_half], 0, across)
    for d in ORDER:
        peer = (q + d) % 8
        send(s_c.at[peer], r_c.at[q], "cq>", ">cq", along_q(peer))
    r_c[pl.ds(q, 1)] = s_c[pl.ds(q, 1)]

    def put(at, x):
        high, low = halves(x)
        lhs[0, at * 64 : (at + 1) * 64] = high
        lhs[1, at * 64 : (at + 1) * 64] = low

    def forward(u, base, stride, out):
        for r in range(0, 8, 2):
            x = [u[pl.ds(base + r + e, 64, stride=stride), :] for e in range(2)]
            x = jnp.concatenate(x, axis=1).astype(BF16)
            a = dot(t_first16[...], jnp.concatenate([x, x], axis=0))
            for e in range(2):
                re = a[:64, e * SIDE : (e + 1) * SIDE]
                im = a[64:, e * SIDE : (e + 1) * SIDE]
                put(r + e, jnp.concatenate([re * cw + im * sw, im * cw - re * sw], axis=1))
        spec[out] = dot(lhs[0], g_high) + (dot(lhs[1], g_high) + dot(lhs[0], g_low))

    def inverse(left, right, conjugate, store):
        for r in range(8):
            rows = slice(r * 64, (r + 1) * 64)
            ar, ai = spec[left, rows, :SIDE], spec[left, rows, SIDE:]
            br, bi = spec[right, rows, :SIDE], spec[right, rows, SIDE:]
            if conjugate:
                p = [ar * br + ai * bi, ar * bi - ai * br]
            else:
                p = [ar * br - ai * bi, ar * bi + ai * br]
            put(r, jnp.concatenate(p, axis=1))
        mid[...] = dot(lhs[0], i_high) + (dot(lhs[1], i_high) + dot(lhs[0], i_low))
        for r in range(0, 8, 2):
            cols = []
            for e in range(2):
                rows = slice((r + e) * 64, (r + e + 1) * 64)
                re, im = mid[rows, :SIDE], mid[rows, SIDE:]
                cols.append(jnp.concatenate([re * cw - im * sw, im * cw + re * sw], axis=0))
            high, low = halves(jnp.concatenate(cols, axis=1))
            y = dot(t_last16[...], jnp.concatenate([high, low, high], axis=0))
            for e in range(2):
                store(r + e, y[:, e * SIDE : (e + 1) * SIDE])

    arrived(r2_e.at[0:7], "eq>", ">eq")
    for qq in range(8):
        x = r2_e[qq].astype(F32)
        for zz in range(8):
            u_e[zz * 64 + qq * 8 : zz * 64 + qq * 8 + 8] = x[zz * 8 : zz * 8 + 8]
    forward(u_e, 0, 8, 0)
    arrived(tk.at[0:3], "tk>", ">tk0")
    give(tk.at[near(2), up_half], tk.at[near(2), up_half], 1, behind)
    give(tk.at[near(3), down_half], tk.at[near(3), down_half], 1, ahead)
    sideways(near(2))
    sideways(near(3))
    for group, (a, b) in enumerate(GROUPS):
        arrived(r2_l.at[0:7, a:b], "lz>", f">lz{group}")
        for slot in range(a, b):
            for zz in range(8):
                at = pl.multiple_of(zz * SIDE + near(slot) * 16, 16)
                u_l[pl.ds(at, 16), :] = r2_l[zz, slot].astype(F32)
    forward(u_l, 8, 16, 2)
    forward(u_l, 0, 16, 1)

    def store_v(r, y):
        w_vg[pl.ds(r, 64, stride=16), :] = y

    def store_g(r, y):
        w_vg[pl.ds(8 + r, 64, stride=16), :] = y

    def store_f(r, y):
        w_f[pl.ds(r, 64, stride=8), :] = y

    inverse(0, 2, True, store_v)
    inverse(0, 1, False, store_g)
    for zz in range(8):
        s3[zz] = w_vg[zz * SIDE : (zz + 1) * SIDE].astype(BF16)
    for ds, mark in ((FAR, "f"), (CLOSE, "c")):
        for d in ds:
            peer = (z + d) % 8
            send(s3.at[peer], r3.at[z], "vz>", ">vz" + mark, along_z(peer))
    r3[pl.ds(z, 1)] = s3[pl.ds(z, 1)]
    inverse(1, 2, True, store_f)
    for zz in range(8):
        s3f[zz] = w_f[zz * 64 : (zz + 1) * 64].astype(BF16)
    arrived(tk.at[0], "tk>", ">tk1")
    sideways(near(6))

    arrived(r_c.at[0:7], "cq>", ">cq")
    wide_c[...] = r_c[...].astype(F32)

    def gate(at):
        x = r3[pl.ds(at, 1)].astype(F32).reshape(8, 16, SIDE)
        factor = wide_c[:, pl.ds(pl.multiple_of(at * 8, 8), 8), :]
        x = jnp.concatenate([x[:, :8], x[:, 8:] * factor], axis=1)
        r3[pl.ds(at, 1)] = x.astype(BF16).reshape(1, SIDE, SIDE)

    gate(z)
    send(r3.at[z], r3s.at[z], "sib>", ">sibc", (i, sib))
    for ds, mark in ((CLOSE, "c"), (FAR, "f")):
        arrived(r3.at[0 : len(ds)], "vz>", ">vz" + mark)
        for d in ds:
            peer = (z + d) % 8
            gate(peer)
            send(r3.at[peer], r3s.at[peer], "sib>", ">sib" + mark, (i, sib))
    for d in ORDER:
        peer = (q + d) % 8
        send(rows16(r3, peer), r4.at[q], "vq>", ">vq", along_q(peer))
    r4[pl.ds(q, 1)] = r3[:, pl.ds(pl.multiple_of(q * 16, 16), 16), :].reshape(1, 8, 16, SIDE)

    for d in ORDER:
        peer = (z + d) % 8
        send(s3f.at[peer], r3f.at[z], "fz>", ">fz", along_z(peer))
    r3f[pl.ds(z, 1)] = s3f[pl.ds(z, 1)]

    for qq in range(8):
        g_all[0:SIDE, qq * SIDE : (qq + 1) * SIDE] = r3[:, qq * 16 : (qq + 1) * 16, :].reshape(SIDE, SIDE)
    arrived(tk.at[0:3], "tk>", ">tk2")
    own.wait()
    arrived(r3s.at[0:5], "sib>", ">sibc")
    arrived(r3s.at[0:3], "sib>", ">sibf")
    for qq in range(8):
        g_all[SIDE:, qq * SIDE : (qq + 1) * SIDE] = r3s[:, qq * 16 : (qq + 1) * 16, :].reshape(SIDE, SIDE)
    for t in range(4):
        sums = dot(g_all[...], tk[:, :, t * 256 : (t + 1) * 256].reshape(1024, 256)).reshape(2, 8, 2, 8, 256)
        to = core * 4 + t
        for s, who in enumerate((c, sib)):
            rows = [sums[s, :, f].reshape(64, 256) for f in range(2)]
            at = (2 * t + s) * 8
            part[at : at + 8] = jnp.concatenate(rows, axis=0).T.astype(BF16).reshape(8, 32, SIDE)

            def share(slot, at=at, to=to, who=who):
                peer = near(slot)
                send(part.at[at + peer], r5.at[z * 8 + q], "rs>", ">rs", (to * 8 + peer, who))

            if s == 1:
                share(0)
            else:

                @pl.when(to != z)
                def _(share=share):
                    share(0)

                @pl.when(to == z)
                def _(at=at):
                    r5[pl.ds(z * 8 + q, 1)] = part[pl.ds(at + q, 1)]

            for slot in range(1, 8):
                share(slot)

    arrived(r4.at[0:7], "vq>", ">vq")
    for qq in range(8):
        x = r4[qq].astype(F32)
        vt[:, qq * 64 : (qq + 1) * 64] = x[:, :8].reshape(64, SIDE).T.astype(BF16)
        gt[:, qq * 64 : (qq + 1) * 64] = x[:, 8:].reshape(64, SIDE).T.astype(BF16)

    def columns(k):
        rows = pl.ds(pl.multiple_of(k * 512, 512), 512)
        over = (((1,), (1,)), ((), ()))
        a = lax.dot_general(vt[...], vw[rows, :], over, preferred_element_type=F32)
        return a + lax.dot_general(gt[...], gw[rows, :], over, preferred_element_type=F32)

    s7[0] = columns(2 * (1 - xh) + 1 - core)
    s7[1] = columns(2 * xh + 1 - core)
    send(s7, r7, "core>", ">core", (i, sib))
    far = columns(2 * (1 - xh) + core)
    here = columns(2 * xh + core)
    arrived(r7, "core>", ">core")
    s8[...] = (far + r7[0]).astype(BF16)
    send(s8, r8, "far>", ">far", (i, opp))
    here = here + r7[1]

    arrived(r3f.at[0:7], "fz>", ">fz")
    regroup(r3f, s4f)
    for d in ORDER:
        peer = (q + d) % 8
        send(s4f.at[peer], r4f.at[q], "fq>", ">fq", along_q(peer))
    r4f[pl.ds(q, 1)] = s4f[pl.ds(q, 1)]

    outs = [
        pltpu.make_async_copy(a, b, sem(f"out{t}"))
        for t, (a, b) in enumerate(zip((o_in, o_fil, o_vw, o_gw), (input_grad, filter_grad, vw_grad, gw_grad)))
    ]
    arrived(r8, "far>", ">far")
    o_in[...] = (here + r8[...].astype(F32)).astype(BF16)
    outs[0].start()
    arrived(r4f.at[0:7], "fq>", ">fq")
    for b in range(4):
        x = r4f[2 * b : 2 * b + 2].astype(F32).reshape(SIDE, SIDE)
        o_fil[:, b * SIDE : (b + 1) * SIDE] = x.T * SCALE
    outs[1].start()

    @pl.when(core == z // 4)
    def _():
        waiter(r5.at[0:63], "rs>", ">rs").wait()

    @pl.when(core != z // 4)
    def _():
        waiter(r5, "rs>", ">rs").wait()

    for qq in range(8):
        total = r5[qq].astype(F32)
        for zz in range(1, 8):
            total = total + r5[zz * 8 + qq].astype(F32)
        total = total * SCALE
        o_vw[:, qq * 64 : (qq + 1) * 64] = total[:, :64]
        o_gw[:, qq * 64 : (qq + 1) * 64] = total[:, 64:]
    outs[2].start()
    outs[3].start()

    for size, out in (
        (r1_e.at[0:7], "ez>"), (r2_e.at[0:7], "eq>"), (r1_l.at[0:7], "lq>"), (r2_l.at[0:7], "lz>"),
        (r3.at[0:7], "vz>"), (r_c.at[0:7], "cq>"), (r3s, "sib>"), (r3f.at[0:7], "fz>"), (r4.at[0:7], "vq>"), (r4f.at[0:7], "fq>"),
        (tk.at[0:7], "tk>"), (r7, "core>"), (r8, "far>"),
    ):
        waiter(size, out, ">ez").wait_send()
    for copy in outs:
        copy.wait()


def local(tokens, value_weight, gate_weight, filters, cotangent):
    def v(*shape, dtype=BF16):
        return pltpu.VMEM(shape, dtype)

    whole = pl.BlockSpec(memory_space=pl.ANY)
    operands = [tokens, value_weight, gate_weight, filters, cotangent]
    operands += [jnp.asarray(t) for t in tables()]
    shape = jax.ShapeDtypeStruct
    outputs = (shape((128, 512), BF16), shape((128, 512), F32), shape((32, 512), F32), shape((32, 512), F32))
    results = pl.pallas_call(
        kernel,
        out_shape=outputs,
        in_specs=[whole] * 9,
        out_specs=(whole,) * 4,
        scratch_shapes=[pltpu.VMEM(t.shape, t.dtype) for t in operands] + [
            v(128, 128), v(4, 256, 256), v(64, 384),
            v(8, 64, 128), v(8, 128, 128), v(8, 64, 128), v(8, 128, 128),
            v(8, 64, 128), v(8, 64, 128), v(8, 8, 16, 128),
            v(512, 128, dtype=F32), v(1024, 128, dtype=F32), v(1024, 128, dtype=F32), v(512, 128, dtype=F32),
            v(8, 64, 128), v(8, 64, 128), v(8, 64, 128, dtype=F32),
            v(3, 512, 256, dtype=F32), v(2, 512, 256), v(512, 256, dtype=F32),
            v(8, 128, 128), v(8, 128, 128), v(8, 128, 128), v(8, 8, 16, 128),
            v(8, 64, 128), v(8, 64, 128), v(8, 64, 128), v(8, 64, 128),
            v(8, 128, 1024), v(256, 1024), v(64, 32, 128), v(64, 32, 128),
            v(128, 512), v(128, 512),
            v(2, 128, 512, dtype=F32), v(2, 128, 512, dtype=F32), v(128, 512), v(128, 512),
        ] + [pltpu.VMEM(t.shape, t.dtype) for t in outputs] + [pltpu.SemaphoreType.DMA((len(SEMAPHORES),))],
        compiler_params=pltpu.CompilerParams(
            collective_id=0, has_side_effects=True, vmem_limit_bytes=60 * 1024 * 1024
        ),
        cost_estimate=pl.CostEstimate(flops=3_000_000_000, bytes_accessed=8_000_000, transcendentals=0),
    )(*operands)
    return pl.pallas_call(
        hand_over,
        out_shape=tuple(shape(r.shape, r.dtype) for r in results),
        in_specs=[whole] * 4,
        out_specs=(whole,) * 4,
        scratch_shapes=[pltpu.VMEM(r.shape, r.dtype) for r in results] + [pltpu.SemaphoreType.DMA((8,))],
        compiler_params=pltpu.CompilerParams(vmem_limit_bytes=60 * 1024 * 1024),
    )(*results)


def hand_over(*refs):
    into = [pltpu.make_async_copy(refs[t], refs[8 + t], refs[12].at[t]) for t in range(4)]
    onto = [pltpu.make_async_copy(refs[8 + t], refs[4 + t], refs[12].at[4 + t]) for t in range(4)]
    for copy in into:
        copy.start()
    for copy, after in zip(into, onto):
        copy.wait()
        after.start()
    for copy in onto:
        copy.wait()


def solution(mesh):
    placed = (P("seq", None), P(None, "ch"), P(None, "ch"), P("seq", "ch"), P("seq", "ch"))
    return jax.shard_map(
        local,
        mesh=mesh,
        in_specs=placed,
        out_specs=(P("seq", "ch"),) * 4,
        check_vma=False,
    )
```

```python
import functools
import math

import jax
import jax.numpy as jnp
import ml_dtypes
import numpy as np
from jax import lax
from jax.experimental import pallas as pl
from jax.experimental.pallas import tpu as pltpu
from jax.sharding import PartitionSpec as P

MESH = pl.DeviceIdType.MESH
F32 = jnp.float32
BF16 = jnp.bfloat16
SIDE = 128
PADDED = SIDE * SIDE
SEQ = PADDED // 2
SCALE = SEQ**-0.5
ORDER = (4, 3, 5, 2, 6, 1, 7)
NEAR = ((0, 0), (1, 0), (0, 1), (0, 3), (1, 1), (1, 3), (0, 2), (1, 2))
BACK = (0, 1, 3, 2, 5, 4, 6, 7)
GROUPS = ((0, 1), (1, 4), (4, 8))
CLOSE, FAR = (2, 6, 1, 7), (4, 3, 5)
LOADS = ("fil", "cot", "tok", "vw", "gw", "first", "twist", "second", "last")
OUTGOING = ("ez", "eq", "lq", "lz", "cq", "vz", "sib", "fz", "vq", "fq", "tk", "rs", "core", "far")
INCOMING = (
    "ez", "eq", "lq1", "lq2", "lz0", "lz1", "lz2", "cq", "vzc", "vzf", "sibc", "sibf", "fz", "vq", "fq",
    "tk0", "tk1", "tk2", "rs", "core", "far",
)
SEMAPHORES = (
    tuple(t + ">" for t in OUTGOING)
    + tuple(">" + t for t in INCOMING)
    + ("own", "self", "out0", "out1")
    + LOADS
)


def split(table):
    high = table.astype(ml_dtypes.bfloat16)
    low = (table - high.astype(np.float64)).astype(ml_dtypes.bfloat16)
    return high, low


def tables():
    half = np.arange(64) + 0.5
    block = 2 * math.pi * np.outer(half, np.arange(64)) / SIDE
    first = np.concatenate([np.cos(block), -np.sin(block)], axis=0)
    first = np.concatenate(split(first), axis=1)
    twist = 2 * math.pi * np.outer(half, np.arange(SIDE)) / PADDED
    twist = np.concatenate([np.cos(twist), np.sin(twist)], axis=0).astype(np.float32)
    inner = 2 * math.pi * np.outer(np.arange(SIDE), np.arange(SIDE)) / SIDE
    c, s = np.cos(inner), np.sin(inner)
    forward = np.block([[c, -s], [s, c]])
    inverse = np.block([[c, s], [-s, c]])
    second = np.concatenate(split(forward) + split(inverse), axis=0)
    last = np.concatenate([np.cos(block.T), -np.sin(block.T)], axis=1) * (2.0 / PADDED)
    high, low = split(last)
    last = np.concatenate([high, high, low], axis=1)
    return tuple(t.astype(np.float32) for t in (first, twist, second, last))


def dot(a, b):
    return jnp.dot(a, b, preferred_element_type=F32)


def halves(x):
    high = x.astype(BF16)
    return high, (x - high.astype(F32)).astype(BF16)


def kernel(
    tok_in, vw_in, gw_in, fil_in, cot_in, t_first_in, t_twist_in, t_second_in, t_last_in,
    input_grad, filter_grad, r5,
    tok, vw, gw, fil, cot, t_first, t_twist, t_second, t_last,
    t_first16, t_second16, t_last16, s_e, s_l, r1_e, r1_l, s2_e, r2_e, r2_l, u_e, u_l, w_vg, w_f,
    s_c, r_c, wide_c,
    spec, lhs, mid, s3, r3, r3s, r4, s3f, r3f, s4f, r4f,
    tk, g_all, part, vt, gt, s7, r7, s8, r8, o_in, o_fil, sems,
):
    i = lax.axis_index("seq")
    c = lax.axis_index("ch")
    z, q = i // 8, i % 8
    core, xh = c % 2, c // 2
    sib = c + 1 - 2 * core
    opp = (c + 2) % 4

    def along_z(zz):
        return (zz * 8 + q, c)

    def along_q(qq):
        return (z * 8 + qq, c)

    def near(slot):
        dx, dy = NEAR[slot]
        return (q // 4 + dx) % 2 * 4 + (q + dy) % 4

    def sem(name):
        return sems.at[SEMAPHORES.index(name)]

    loads = {}
    sources = (fil_in, cot_in, tok_in, vw_in, gw_in, t_first_in, t_twist_in, t_second_in, t_last_in)
    places = (fil, cot, tok, vw, gw, t_first, t_twist, t_second, t_last)
    for name, src, dst in zip(LOADS, sources, places):
        loads[name] = pltpu.make_async_copy(src, dst, sem(name))
        loads[name].start()

    barrier = pltpu.get_barrier_semaphore()
    peers = 0
    for d in range(1, 8):
        for who in (along_z((z + d) % 8), along_q((q + d) % 8)):
            pl.semaphore_signal(barrier, inc=1, device_id=who, device_id_type=MESH)
            peers += 1
    for who in ((i, sib), (i, opp), (along_q(near(1))[0], opp)):
        pl.semaphore_signal(barrier, inc=1, device_id=who, device_id_type=MESH)
        peers += 1

    def pair(a, b):
        a = a.T.reshape(16, 8, SIDE)
        b = b.T.reshape(16, 8, SIDE)
        return jnp.concatenate([a, b], axis=1).astype(BF16).reshape(2, SIDE, SIDE)

    def send(src, dst, out, into, who):
        pltpu.make_async_remote_copy(
            src_ref=src, dst_ref=dst, send_sem=sem(out), recv_sem=sem(into), device_id=who, device_id_type=MESH
        ).start()

    def waiter(size, out, into):
        return pltpu.make_async_remote_copy(
            src_ref=size, dst_ref=size, send_sem=sem(out), recv_sem=sem(into),
            device_id=(i, sib), device_id_type=MESH,
        )

    def arrived(size, out, into):
        waiter(size, out, into).wait_recv()

    def rows16(ref, at):
        return ref.at[:, pl.ds(pl.multiple_of(at * 16, 16), 16), :]

    loads["fil"].wait()
    for b in range(4):
        rows = fil[:, b * SIDE : (b + 1) * SIDE].T.reshape(2, 8, 8, SIDE)
        for zz in range(8):
            s_e[zz, b * 16 : (b + 1) * 16] = rows[:, zz].reshape(16, SIDE).astype(BF16)
    loads["tok"].wait()
    own_cols = pl.ds(pl.multiple_of(core * 1024, 1024), 1024)
    half = tok.at[:, own_cols]
    own = pltpu.make_async_copy(half, tk.at[q], sem("own"))
    own.start()

    pl.semaphore_wait(barrier, peers)
    for d in ORDER:
        peer = (z + d) % 8
        send(s_e.at[peer], r1_e.at[z], "ez>", ">ez", along_z(peer))
    r1_e[pl.ds(z, 1)] = s_e[pl.ds(z, 1)]

    loads["cot"].wait()
    loads["vw"].wait()
    loads["gw"].wait()
    for b in range(2):
        lanes = slice(b * 256, (b + 1) * 256)
        val = dot(tok[...], vw[:, lanes])
        up = dot(tok[...], gw[:, lanes]) * cot[:, lanes].astype(F32)
        for e in range(2):
            part_lanes = slice(e * SIDE, (e + 1) * SIDE)
            at = 4 * b + 2 * e
            s_l[at : at + 2] = pair(val[:, part_lanes], up[:, part_lanes])
    for group in (1, 2):
        for slot in range(*GROUPS[group]):
            send(s_l.at[near(slot)], r1_l.at[BACK[slot]], "lq>", f">lq{group}", along_q(near(slot)))
    r1_l[0] = s_l[pl.ds(q, 1)].reshape(SIDE, SIDE)

    def onward(group):
        a, b = GROUPS[group]
        if group:
            arrived(r1_l.at[a:b], "lq>", f">lq{group}")
        for d in ORDER:
            peer = (z + d) % 8
            rows = pl.ds(pl.multiple_of(peer * 16, 16), 16)
            send(r1_l.at[a:b, rows, :], r2_l.at[z, a:b], "lz>", f">lz{group}", along_z(peer))
        mine = r1_l[a:b, pl.ds(pl.multiple_of(z * 16, 16), 16), :]
        r2_l[pl.ds(z, 1), a:b] = mine.reshape(1, b - a, 16, SIDE)

    def give(src, dst, at, who):
        send(src, dst, "tk>", f">tk{at}", who)

    up_half, down_half = slice(0, 64), slice(64, SIDE)
    ahead, behind = along_q(near(2)), along_q(near(3))
    beside, across = along_q(near(1)), (along_q(near(1))[0], opp)

    def sideways(block):
        give(tk.at[block, up_half], tk.at[block, up_half], 2, beside)
        give(tk.at[block, down_half], tk.at[block, down_half], 2, across)

    onward(0)
    for name in ("first", "twist", "second", "last"):
        loads[name].wait()
    cw = t_twist[0:64]
    sw = t_twist[64:128]
    for t in range(4):
        t_second16[t] = t_second[256 * t : 256 * (t + 1)].astype(BF16)
    t_first16[...] = t_first[...].astype(BF16)
    t_last16[...] = t_last[...].astype(BF16)
    g_high, g_low, i_high, i_low = (t_second16[t] for t in range(4))
    for b in range(4):
        lanes = slice(b * SIDE, (b + 1) * SIDE)
        s_c[2 * b : 2 * b + 2] = cot[:, lanes].astype(F32).T.astype(BF16).reshape(2, 64, SIDE)
    onward(1)
    give(half, tk.at[q], 0, ahead)
    give(half, tk.at[q], 0, behind)
    give(tok.at[up_half, own_cols], tk.at[q, up_half], 0, beside)
    give(tok.at[down_half, own_cols], tk.at[q, down_half], 0, across)
    onward(2)

    def regroup(src, dst):
        x = src[...].astype(F32).reshape(8, 8, 8, SIDE)
        for qq in range(8):
            dst[qq] = x[:, qq].reshape(64, SIDE).astype(BF16)

    arrived(r1_e.at[0:7], "ez>", ">ez")
    regroup(r1_e, s2_e)
    for d in ORDER:
        peer = (q + d) % 8
        send(s2_e.at[peer], r2_e.at[q], "eq>", ">eq", along_q(peer))
    r2_e[pl.ds(q, 1)] = s2_e[pl.ds(q, 1)]
    for d in ORDER:
        peer = (q + d) % 8
        send(s_c.at[peer], r_c.at[q], "cq>", ">cq", along_q(peer))
    r_c[pl.ds(q, 1)] = s_c[pl.ds(q, 1)]

    def put(at, x):
        high, low = halves(x)
        lhs[0, at * 64 : (at + 1) * 64] = high
        lhs[1, at * 64 : (at + 1) * 64] = low

    def forward(u, base, stride, out):
        for r in range(0, 8, 2):
            x = [u[pl.ds(base + r + e, 64, stride=stride), :] for e in range(2)]
            x = jnp.concatenate(x, axis=1).astype(BF16)
            a = dot(t_first16[...], jnp.concatenate([x, x], axis=0))
            for e in range(2):
                re = a[:64, e * SIDE : (e + 1) * SIDE]
                im = a[64:, e * SIDE : (e + 1) * SIDE]
                put(r + e, jnp.concatenate([re * cw + im * sw, im * cw - re * sw], axis=1))
        spec[out] = dot(lhs[0], g_high) + (dot(lhs[1], g_high) + dot(lhs[0], g_low))

    def inverse(left, right, conjugate, store):
        for r in range(8):
            rows = slice(r * 64, (r + 1) * 64)
            ar, ai = spec[left, rows, :SIDE], spec[left, rows, SIDE:]
            br, bi = spec[right, rows, :SIDE], spec[right, rows, SIDE:]
            if conjugate:
                p = [ar * br + ai * bi, ar * bi - ai * br]
            else:
                p = [ar * br - ai * bi, ar * bi + ai * br]
            put(r, jnp.concatenate(p, axis=1))
        mid[...] = dot(lhs[0], i_high) + (dot(lhs[1], i_high) + dot(lhs[0], i_low))
        for r in range(0, 8, 2):
            cols = []
            for e in range(2):
                rows = slice((r + e) * 64, (r + e + 1) * 64)
                re, im = mid[rows, :SIDE], mid[rows, SIDE:]
                cols.append(jnp.concatenate([re * cw - im * sw, im * cw + re * sw], axis=0))
            high, low = halves(jnp.concatenate(cols, axis=1))
            y = dot(t_last16[...], jnp.concatenate([high, low, high], axis=0))
            for e in range(2):
                store(r + e, y[:, e * SIDE : (e + 1) * SIDE])

    arrived(r2_e.at[0:7], "eq>", ">eq")
    for qq in range(8):
        x = r2_e[qq].astype(F32)
        for zz in range(8):
            u_e[zz * 64 + qq * 8 : zz * 64 + qq * 8 + 8] = x[zz * 8 : zz * 8 + 8]
    forward(u_e, 0, 8, 0)
    for group, (a, b) in enumerate(GROUPS):
        arrived(r2_l.at[0:7, a:b], "lz>", f">lz{group}")
        for slot in range(a, b):
            for zz in range(8):
                at = pl.multiple_of(zz * SIDE + near(slot) * 16, 16)
                u_l[pl.ds(at, 16), :] = r2_l[zz, slot].astype(F32)
    forward(u_l, 8, 16, 2)
    forward(u_l, 0, 16, 1)

    def store_v(r, y):
        w_vg[pl.ds(r, 64, stride=16), :] = y

    def store_g(r, y):
        w_vg[pl.ds(8 + r, 64, stride=16), :] = y

    def store_f(r, y):
        w_f[pl.ds(r, 64, stride=8), :] = y

    inverse(0, 2, True, store_v)
    inverse(0, 1, False, store_g)
    for zz in range(8):
        s3[zz] = w_vg[zz * SIDE : (zz + 1) * SIDE].astype(BF16)
    for ds, mark in ((FAR, "f"), (CLOSE, "c")):
        for d in ds:
            peer = (z + d) % 8
            send(s3.at[peer], r3.at[z], "vz>", ">vz" + mark, along_z(peer))
    r3[pl.ds(z, 1)] = s3[pl.ds(z, 1)]
    arrived(tk.at[0:3], "tk>", ">tk0")
    give(tk.at[near(2), up_half], tk.at[near(2), up_half], 1, behind)
    give(tk.at[near(3), down_half], tk.at[near(3), down_half], 1, ahead)
    sideways(near(2))
    sideways(near(3))
    inverse(1, 2, True, store_f)
    for zz in range(8):
        s3f[zz] = w_f[zz * 64 : (zz + 1) * 64].astype(BF16)
    arrived(tk.at[0], "tk>", ">tk1")
    sideways(near(6))

    arrived(r_c.at[0:7], "cq>", ">cq")
    wide_c[...] = r_c[...].astype(F32)

    def gate(at):
        x = r3[pl.ds(at, 1)].astype(F32).reshape(8, 16, SIDE)
        factor = wide_c[:, pl.ds(pl.multiple_of(at * 8, 8), 8), :]
        x = jnp.concatenate([x[:, :8], x[:, 8:] * factor], axis=1)
        r3[pl.ds(at, 1)] = x.astype(BF16).reshape(1, SIDE, SIDE)

    gate(z)
    send(r3.at[z], r3s.at[z], "sib>", ">sibc", (i, sib))
    for ds, mark in ((CLOSE, "c"), (FAR, "f")):
        arrived(r3.at[0 : len(ds)], "vz>", ">vz" + mark)
        for d in ds:
            peer = (z + d) % 8
            gate(peer)
            send(r3.at[peer], r3s.at[peer], "sib>", ">sib" + mark, (i, sib))
    for d in ORDER:
        peer = (q + d) % 8
        send(rows16(r3, peer), r4.at[q], "vq>", ">vq", along_q(peer))
    r4[pl.ds(q, 1)] = r3[:, pl.ds(pl.multiple_of(q * 16, 16), 16), :].reshape(1, 8, 16, SIDE)

    for d in ORDER:
        peer = (z + d) % 8
        send(s3f.at[peer], r3f.at[z], "fz>", ">fz", along_z(peer))
    r3f[pl.ds(z, 1)] = s3f[pl.ds(z, 1)]

    for qq in range(8):
        g_all[0:SIDE, qq * SIDE : (qq + 1) * SIDE] = r3[:, qq * 16 : (qq + 1) * 16, :].reshape(SIDE, SIDE)
    arrived(tk.at[0:3], "tk>", ">tk2")
    own.wait()
    arrived(r3s.at[0:5], "sib>", ">sibc")
    arrived(r3s.at[0:3], "sib>", ">sibf")
    for qq in range(8):
        g_all[SIDE:, qq * SIDE : (qq + 1) * SIDE] = r3s[:, qq * 16 : (qq + 1) * 16, :].reshape(SIDE, SIDE)
    for t in range(4):
        sums = dot(g_all[...], tk[:, :, t * 256 : (t + 1) * 256].reshape(1024, 256)).reshape(2, 8, 2, 8, 256)
        to = core * 4 + t
        for s, who in enumerate((c, sib)):
            rows = [sums[s, :, f].reshape(64, 256) for f in range(2)]
            at = (2 * t + s) * 8
            part[at : at + 8] = jnp.concatenate(rows, axis=0).T.astype(BF16).reshape(8, 32, SIDE)

            def share(slot, at=at, to=to, who=who):
                peer = near(slot)
                send(part.at[at + peer], r5.at[z * 8 + q], "rs>", ">rs", (to * 8 + peer, who))

            if s == 1:
                share(0)
            else:

                @pl.when(to != z)
                def _(share=share):
                    share(0)

                @pl.when(to == z)
                def _(at=at):
                    pltpu.make_async_copy(part.at[at + q], r5.at[z * 8 + q], sem("self")).start()

            for slot in range(1, 8):
                share(slot)

    arrived(r4.at[0:7], "vq>", ">vq")
    for qq in range(8):
        x = r4[qq].astype(F32)
        vt[:, qq * 64 : (qq + 1) * 64] = x[:, :8].reshape(64, SIDE).T.astype(BF16)
        gt[:, qq * 64 : (qq + 1) * 64] = x[:, 8:].reshape(64, SIDE).T.astype(BF16)

    def columns(k):
        rows = pl.ds(pl.multiple_of(k * 512, 512), 512)
        over = (((1,), (1,)), ((), ()))
        a = lax.dot_general(vt[...], vw[rows, :], over, preferred_element_type=F32)
        return a + lax.dot_general(gt[...], gw[rows, :], over, preferred_element_type=F32)

    s7[0] = columns(2 * (1 - xh) + 1 - core)
    s7[1] = columns(2 * xh + 1 - core)
    send(s7, r7, "core>", ">core", (i, sib))
    far = columns(2 * (1 - xh) + core)
    here = columns(2 * xh + core)
    arrived(r7, "core>", ">core")
    s8[...] = (far + r7[0]).astype(BF16)
    send(s8, r8, "far>", ">far", (i, opp))
    here = here + r7[1]

    arrived(r3f.at[0:7], "fz>", ">fz")
    regroup(r3f, s4f)
    for d in ORDER:
        peer = (q + d) % 8
        send(s4f.at[peer], r4f.at[q], "fq>", ">fq", along_q(peer))
    r4f[pl.ds(q, 1)] = s4f[pl.ds(q, 1)]

    outs = [
        pltpu.make_async_copy(a, b, sem(f"out{t}"))
        for t, (a, b) in enumerate(zip((o_in, o_fil), (input_grad, filter_grad)))
    ]
    arrived(r8, "far>", ">far")
    o_in[...] = (here + r8[...].astype(F32)).astype(BF16)
    outs[0].start()
    arrived(r4f.at[0:7], "fq>", ">fq")
    for b in range(4):
        x = r4f[2 * b : 2 * b + 2].astype(F32).reshape(SIDE, SIDE)
        o_fil[:, b * SIDE : (b + 1) * SIDE] = x.T * SCALE
    outs[1].start()

    @pl.when(core == z // 4)
    def _():
        waiter(r5.at[0:63], "rs>", ">rs").wait()
        pltpu.make_async_copy(part.at[0], r5.at[0], sem("self")).wait()

    @pl.when(core != z // 4)
    def _():
        waiter(r5, "rs>", ">rs").wait()

    for size, out in (
        (r1_e.at[0:7], "ez>"), (r2_e.at[0:7], "eq>"), (r1_l.at[0:7], "lq>"), (r2_l.at[0:7], "lz>"),
        (r3.at[0:7], "vz>"), (r_c.at[0:7], "cq>"), (r3s, "sib>"), (r3f.at[0:7], "fz>"), (r4.at[0:7], "vq>"), (r4f.at[0:7], "fq>"),
        (tk.at[0:7], "tk>"), (r7, "core>"), (r8, "far>"),
    ):
        waiter(size, out, ">ez").wait_send()
    for copy in outs:
        copy.wait()


def local(tokens, value_weight, gate_weight, filters, cotangent):
    def v(*shape, dtype=BF16):
        return pltpu.VMEM(shape, dtype)

    whole = pl.BlockSpec(memory_space=pl.ANY)
    operands = [tokens, value_weight, gate_weight, filters, cotangent]
    operands += [jnp.asarray(t) for t in tables()]
    shape = jax.ShapeDtypeStruct
    input_grad, filter_grad = shape((128, 512), BF16), shape((128, 512), F32)
    weight_grad, terms = shape((32, 512), F32), shape((64, 32, 128), BF16)
    results = pl.pallas_call(
        kernel,
        out_shape=(input_grad, filter_grad, terms),
        in_specs=[whole] * 9,
        out_specs=(whole,) * 3,
        scratch_shapes=[pltpu.VMEM(t.shape, t.dtype) for t in operands] + [
            v(128, 128), v(4, 256, 256), v(64, 384),
            v(8, 64, 128), v(8, 128, 128), v(8, 64, 128), v(8, 128, 128),
            v(8, 64, 128), v(8, 64, 128), v(8, 8, 16, 128),
            v(512, 128, dtype=F32), v(1024, 128, dtype=F32), v(1024, 128, dtype=F32), v(512, 128, dtype=F32),
            v(8, 64, 128), v(8, 64, 128), v(8, 64, 128, dtype=F32),
            v(3, 512, 256, dtype=F32), v(2, 512, 256), v(512, 256, dtype=F32),
            v(8, 128, 128), v(8, 128, 128), v(8, 128, 128), v(8, 8, 16, 128),
            v(8, 64, 128), v(8, 64, 128), v(8, 64, 128), v(8, 64, 128),
            v(8, 128, 1024), v(256, 1024), v(64, 32, 128),
            v(128, 512), v(128, 512),
            v(2, 128, 512, dtype=F32), v(2, 128, 512, dtype=F32), v(128, 512), v(128, 512),
        ] + [pltpu.VMEM(t.shape, t.dtype) for t in (input_grad, filter_grad)] + [pltpu.SemaphoreType.DMA((len(SEMAPHORES),))],
        compiler_params=pltpu.CompilerParams(
            collective_id=0, has_side_effects=True, vmem_limit_bytes=60 * 1024 * 1024
        ),
        cost_estimate=pl.CostEstimate(flops=3_000_000_000, bytes_accessed=8_000_000, transcendentals=0),
    )(*operands)
    outputs = (input_grad, filter_grad, weight_grad, weight_grad)
    return pl.pallas_call(
        finish,
        out_shape=outputs,
        in_specs=[whole] * 3,
        out_specs=(whole,) * 4,
        scratch_shapes=[pltpu.VMEM(t.shape, t.dtype) for t in outputs + (terms,)] + [pltpu.SemaphoreType.DMA((7,))],
        compiler_params=pltpu.CompilerParams(vmem_limit_bytes=60 * 1024 * 1024),
    )(*results)


def finish(
    in_grad_in, filter_grad_in, terms_in, in_grad, filter_grad, vw_grad, gw_grad,
    o_in, o_fil, o_vw, o_gw, terms, sems,
):
    loads = [
        pltpu.make_async_copy(a, b, sems.at[t])
        for t, (a, b) in enumerate(((terms_in, terms), (in_grad_in, o_in), (filter_grad_in, o_fil)))
    ]
    for load in loads:
        load.start()
    stores = [
        pltpu.make_async_copy(a, b, sems.at[3 + t])
        for t, (a, b) in enumerate(((o_in, in_grad), (o_fil, filter_grad), (o_vw, vw_grad), (o_gw, gw_grad)))
    ]
    loads[0].wait()
    for qq in range(8):
        total = terms[qq].astype(F32)
        for zz in range(1, 8):
            total = total + terms[zz * 8 + qq].astype(F32)
        total = total * SCALE
        o_vw[:, qq * 64 : (qq + 1) * 64] = total[:, :64]
        o_gw[:, qq * 64 : (qq + 1) * 64] = total[:, 64:]
    stores[2].start()
    stores[3].start()
    for t in (1, 2):
        loads[t].wait()
        stores[t - 1].start()
    for store in stores:
        store.wait()


def solution(mesh):
    placed = (P("seq", None), P(None, "ch"), P(None, "ch"), P("seq", "ch"), P("seq", "ch"))
    return jax.shard_map(
        local,
        mesh=mesh,
        in_specs=placed,
        out_specs=(P("seq", "ch"),) * 4,
        check_vma=False,
    )
```

```python
import functools
import math

import jax
import jax.numpy as jnp
import ml_dtypes
import numpy as np
from jax import lax
from jax.experimental import pallas as pl
from jax.experimental.pallas import tpu as pltpu
from jax.sharding import PartitionSpec as P

MESH = pl.DeviceIdType.MESH
F32 = jnp.float32
BF16 = jnp.bfloat16
SIDE = 128
PADDED = SIDE * SIDE
SEQ = PADDED // 2
SCALE = SEQ**-0.5
ORDER = (4, 3, 5, 2, 6, 1, 7)
NEAR = ((0, 0), (1, 0), (0, 1), (0, 3), (1, 1), (1, 3), (0, 2), (1, 2))
BACK = (0, 1, 3, 2, 5, 4, 6, 7)
GROUPS = ((0, 1), (1, 4), (4, 8))
CLOSE, FAR = (2, 6, 1, 7), (4, 3, 5)
LOADS = ("fil", "cot", "tok", "vw", "gw", "first", "twist", "second", "last")
OUTGOING = ("ez", "eq", "lq", "lz", "cq", "vz", "sib", "fz", "vq", "fq", "tk", "rs", "core", "far")
INCOMING = (
    "ez", "eq", "lq1", "lq2", "lz0", "lz1", "lz2", "cq", "vzc", "vzf", "sibc", "sibf", "fz", "vq", "fq",
    "tk0", "tk1", "tk2", "rs", "core", "far",
)
SEMAPHORES = (
    tuple(t + ">" for t in OUTGOING)
    + tuple(">" + t for t in INCOMING)
    + ("own", "self", "out0", "out1")
    + LOADS
)


def split(table):
    high = table.astype(ml_dtypes.bfloat16)
    low = (table - high.astype(np.float64)).astype(ml_dtypes.bfloat16)
    return high, low


def tables():
    half = np.arange(64) + 0.5
    block = 2 * math.pi * np.outer(half, np.arange(64)) / SIDE
    first = np.concatenate([np.cos(block), -np.sin(block)], axis=0)
    first = np.concatenate(split(first), axis=1)
    twist = 2 * math.pi * np.outer(half, np.arange(SIDE)) / PADDED
    twist = np.concatenate([np.cos(twist), np.sin(twist)], axis=0).astype(np.float32)
    inner = 2 * math.pi * np.outer(np.arange(SIDE), np.arange(SIDE)) / SIDE
    c, s = np.cos(inner), np.sin(inner)
    forward = np.block([[c, -s], [s, c]])
    inverse = np.block([[c, s], [-s, c]])
    second = np.concatenate(split(forward) + split(inverse), axis=0)
    last = np.concatenate([np.cos(block.T), -np.sin(block.T)], axis=1) * (2.0 / PADDED)
    high, low = split(last)
    last = np.concatenate([high, high, low], axis=1)
    return tuple(t.astype(np.float32) for t in (first, twist, second, last))


def dot(a, b):
    return jnp.dot(a, b, preferred_element_type=F32)


def halves(x):
    high = x.astype(BF16)
    return high, (x - high.astype(F32)).astype(BF16)


def kernel(
    tok_in, vw_in, gw_in, fil_in, cot_in, t_first_in, t_twist_in, t_second_in, t_last_in,
    input_grad, filter_grad, r5,
    tok, vw, gw, fil, cot, t_first, t_twist, t_second, t_last,
    t_first16, t_second16, t_last16, s_e, s_l, r1_e, r1_l, s2_e, r2_e, r2_l, u_e, u_l, w_vg, w_f,
    s_c, r_c, wide_c,
    spec, lhs, mid, s3, r3, r3s, r4, s3f, r3f, s4f, r4f,
    tk, g_all, part, vt, gt, s7, r7, s8, r8, o_in, o_fil, sems,
):
    i = lax.axis_index("seq")
    c = lax.axis_index("ch")
    z, q = i // 8, i % 8
    core, xh = c % 2, c // 2
    sib = c + 1 - 2 * core
    opp = (c + 2) % 4

    def along_z(zz):
        return (zz * 8 + q, c)

    def along_q(qq):
        return (z * 8 + qq, c)

    def near(slot):
        dx, dy = NEAR[slot]
        return (q // 4 + dx) % 2 * 4 + (q + dy) % 4

    def sem(name):
        return sems.at[SEMAPHORES.index(name)]

    loads = {}
    sources = (fil_in, cot_in, tok_in, vw_in, gw_in, t_first_in, t_twist_in, t_second_in, t_last_in)
    places = (fil, cot, tok, vw, gw, t_first, t_twist, t_second, t_last)
    for name, src, dst in zip(LOADS, sources, places):
        loads[name] = pltpu.make_async_copy(src, dst, sem(name))
        loads[name].start()

    barrier = pltpu.get_barrier_semaphore()
    peers = 0
    for d in range(1, 8):
        for who in (along_z((z + d) % 8), along_q((q + d) % 8)):
            pl.semaphore_signal(barrier, inc=1, device_id=who, device_id_type=MESH)
            peers += 1
    for who in ((i, sib), (i, opp), (along_q(near(1))[0], opp)):
        pl.semaphore_signal(barrier, inc=1, device_id=who, device_id_type=MESH)
        peers += 1

    def pair(a, b):
        a = a.T.reshape(16, 8, SIDE)
        b = b.T.reshape(16, 8, SIDE)
        return jnp.concatenate([a, b], axis=1).astype(BF16).reshape(2, SIDE, SIDE)

    def send(src, dst, out, into, who):
        pltpu.make_async_remote_copy(
            src_ref=src, dst_ref=dst, send_sem=sem(out), recv_sem=sem(into), device_id=who, device_id_type=MESH
        ).start()

    def waiter(size, out, into):
        return pltpu.make_async_remote_copy(
            src_ref=size, dst_ref=size, send_sem=sem(out), recv_sem=sem(into),
            device_id=(i, sib), device_id_type=MESH,
        )

    def arrived(size, out, into):
        waiter(size, out, into).wait_recv()

    def rows16(ref, at):
        return ref.at[:, pl.ds(pl.multiple_of(at * 16, 16), 16), :]

    loads["fil"].wait()
    for b in range(4):
        rows = fil[:, b * SIDE : (b + 1) * SIDE].T.reshape(2, 8, 8, SIDE)
        for zz in range(8):
            s_e[zz, b * 16 : (b + 1) * 16] = rows[:, zz].reshape(16, SIDE).astype(BF16)
    loads["tok"].wait()
    own_cols = pl.ds(pl.multiple_of(core * 1024, 1024), 1024)
    half = tok.at[:, own_cols]
    own = pltpu.make_async_copy(half, tk.at[q], sem("own"))
    own.start()

    def give(src, dst, at, who):
        send(src, dst, "tk>", f">tk{at}", who)

    up_half, down_half = slice(0, 64), slice(64, SIDE)
    ahead, behind = along_q(near(2)), along_q(near(3))
    beside, across = along_q(near(1)), (along_q(near(1))[0], opp)

    def sideways(block):
        give(tk.at[block, up_half], tk.at[block, up_half], 2, beside)
        give(tk.at[block, down_half], tk.at[block, down_half], 2, across)

    def pieces(first, last):
        for k in range(first, last):
            rows = slice(16 * k, 16 * (k + 1))
            for who in (ahead, behind, beside if k < 4 else across):
                give(tok.at[rows, own_cols], tk.at[q, rows], 0, who)

    pl.semaphore_wait(barrier, peers)
    for d in ORDER:
        peer = (z + d) % 8
        send(s_e.at[peer], r1_e.at[z], "ez>", ">ez", along_z(peer))
    r1_e[pl.ds(z, 1)] = s_e[pl.ds(z, 1)]

    pieces(0, 2)
    loads["cot"].wait()
    loads["vw"].wait()
    loads["gw"].wait()
    for b in range(2):
        lanes = slice(b * 256, (b + 1) * 256)
        val = dot(tok[...], vw[:, lanes])
        up = dot(tok[...], gw[:, lanes]) * cot[:, lanes].astype(F32)
        for e in range(2):
            part_lanes = slice(e * SIDE, (e + 1) * SIDE)
            at = 4 * b + 2 * e
            s_l[at : at + 2] = pair(val[:, part_lanes], up[:, part_lanes])
    for group in (1, 2):
        for slot in range(*GROUPS[group]):
            send(s_l.at[near(slot)], r1_l.at[BACK[slot]], "lq>", f">lq{group}", along_q(near(slot)))
    r1_l[0] = s_l[pl.ds(q, 1)].reshape(SIDE, SIDE)

    pieces(2, 4)
    def onward(group):
        a, b = GROUPS[group]
        if group:
            arrived(r1_l.at[a:b], "lq>", f">lq{group}")
        for d in ORDER:
            peer = (z + d) % 8
            rows = pl.ds(pl.multiple_of(peer * 16, 16), 16)
            send(r1_l.at[a:b, rows, :], r2_l.at[z, a:b], "lz>", f">lz{group}", along_z(peer))
        mine = r1_l[a:b, pl.ds(pl.multiple_of(z * 16, 16), 16), :]
        r2_l[pl.ds(z, 1), a:b] = mine.reshape(1, b - a, 16, SIDE)

    onward(0)
    for name in ("first", "twist", "second", "last"):
        loads[name].wait()
    cw = t_twist[0:64]
    sw = t_twist[64:128]
    for t in range(4):
        t_second16[t] = t_second[256 * t : 256 * (t + 1)].astype(BF16)
    t_first16[...] = t_first[...].astype(BF16)
    t_last16[...] = t_last[...].astype(BF16)
    g_high, g_low, i_high, i_low = (t_second16[t] for t in range(4))
    for b in range(4):
        lanes = slice(b * SIDE, (b + 1) * SIDE)
        s_c[2 * b : 2 * b + 2] = cot[:, lanes].astype(F32).T.astype(BF16).reshape(2, 64, SIDE)
    onward(1)
    pieces(4, 5)
    onward(2)

    pieces(5, 6)
    def regroup(src, dst):
        x = src[...].astype(F32).reshape(8, 8, 8, SIDE)
        for qq in range(8):
            dst[qq] = x[:, qq].reshape(64, SIDE).astype(BF16)

    arrived(r1_e.at[0:7], "ez>", ">ez")
    regroup(r1_e, s2_e)
    for d in ORDER:
        peer = (q + d) % 8
        send(s2_e.at[peer], r2_e.at[q], "eq>", ">eq", along_q(peer))
    r2_e[pl.ds(q, 1)] = s2_e[pl.ds(q, 1)]
    pieces(6, 8)
    for d in ORDER:
        peer = (q + d) % 8
        send(s_c.at[peer], r_c.at[q], "cq>", ">cq", along_q(peer))
    r_c[pl.ds(q, 1)] = s_c[pl.ds(q, 1)]

    def put(at, x):
        high, low = halves(x)
        lhs[0, at * 64 : (at + 1) * 64] = high
        lhs[1, at * 64 : (at + 1) * 64] = low

    def forward(u, base, stride, out):
        for r in range(0, 8, 2):
            x = [u[pl.ds(base + r + e, 64, stride=stride), :] for e in range(2)]
            x = jnp.concatenate(x, axis=1).astype(BF16)
            a = dot(t_first16[...], jnp.concatenate([x, x], axis=0))
            for e in range(2):
                re = a[:64, e * SIDE : (e + 1) * SIDE]
                im = a[64:, e * SIDE : (e + 1) * SIDE]
                put(r + e, jnp.concatenate([re * cw + im * sw, im * cw - re * sw], axis=1))
        spec[out] = dot(lhs[0], g_high) + (dot(lhs[1], g_high) + dot(lhs[0], g_low))

    def inverse(left, right, conjugate, store):
        for r in range(8):
            rows = slice(r * 64, (r + 1) * 64)
            ar, ai = spec[left, rows, :SIDE], spec[left, rows, SIDE:]
            br, bi = spec[right, rows, :SIDE], spec[right, rows, SIDE:]
            if conjugate:
                p = [ar * br + ai * bi, ar * bi - ai * br]
            else:
                p = [ar * br - ai * bi, ar * bi + ai * br]
            put(r, jnp.concatenate(p, axis=1))
        mid[...] = dot(lhs[0], i_high) + (dot(lhs[1], i_high) + dot(lhs[0], i_low))
        for r in range(0, 8, 2):
            cols = []
            for e in range(2):
                rows = slice((r + e) * 64, (r + e + 1) * 64)
                re, im = mid[rows, :SIDE], mid[rows, SIDE:]
                cols.append(jnp.concatenate([re * cw - im * sw, im * cw + re * sw], axis=0))
            high, low = halves(jnp.concatenate(cols, axis=1))
            y = dot(t_last16[...], jnp.concatenate([high, low, high], axis=0))
            for e in range(2):
                store(r + e, y[:, e * SIDE : (e + 1) * SIDE])

    arrived(r2_e.at[0:7], "eq>", ">eq")
    for qq in range(8):
        x = r2_e[qq].astype(F32)
        for zz in range(8):
            u_e[zz * 64 + qq * 8 : zz * 64 + qq * 8 + 8] = x[zz * 8 : zz * 8 + 8]
    forward(u_e, 0, 8, 0)
    for group, (a, b) in enumerate(GROUPS):
        arrived(r2_l.at[0:7, a:b], "lz>", f">lz{group}")
        for slot in range(a, b):
            for zz in range(8):
                at = pl.multiple_of(zz * SIDE + near(slot) * 16, 16)
                u_l[pl.ds(at, 16), :] = r2_l[zz, slot].astype(F32)
    arrived(tk.at[0:3], "tk>", ">tk0")
    give(tk.at[near(2), up_half], tk.at[near(2), up_half], 1, behind)
    give(tk.at[near(3), down_half], tk.at[near(3), down_half], 1, ahead)
    sideways(near(2))
    sideways(near(3))
    forward(u_l, 8, 16, 2)
    forward(u_l, 0, 16, 1)

    def store_v(r, y):
        w_vg[pl.ds(r, 64, stride=16), :] = y

    def store_g(r, y):
        w_vg[pl.ds(8 + r, 64, stride=16), :] = y

    def store_f(r, y):
        w_f[pl.ds(r, 64, stride=8), :] = y

    inverse(0, 2, True, store_v)
    inverse(0, 1, False, store_g)
    for zz in range(8):
        s3[zz] = w_vg[zz * SIDE : (zz + 1) * SIDE].astype(BF16)
    for ds, mark in ((FAR, "f"), (CLOSE, "c")):
        for d in ds:
            peer = (z + d) % 8
            send(s3.at[peer], r3.at[z], "vz>", ">vz" + mark, along_z(peer))
    r3[pl.ds(z, 1)] = s3[pl.ds(z, 1)]
    inverse(1, 2, True, store_f)
    for zz in range(8):
        s3f[zz] = w_f[zz * 64 : (zz + 1) * 64].astype(BF16)

    arrived(tk.at[0], "tk>", ">tk1")
    sideways(near(6))
    arrived(r_c.at[0:7], "cq>", ">cq")
    wide_c[...] = r_c[...].astype(F32)

    def gate(at):
        x = r3[pl.ds(at, 1)].astype(F32).reshape(8, 16, SIDE)
        factor = wide_c[:, pl.ds(pl.multiple_of(at * 8, 8), 8), :]
        x = jnp.concatenate([x[:, :8], x[:, 8:] * factor], axis=1)
        r3[pl.ds(at, 1)] = x.astype(BF16).reshape(1, SIDE, SIDE)

    gate(z)
    send(r3.at[z], r3s.at[z], "sib>", ">sibc", (i, sib))
    for ds, mark in ((CLOSE, "c"), (FAR, "f")):
        arrived(r3.at[0 : len(ds)], "vz>", ">vz" + mark)
        for d in ds:
            peer = (z + d) % 8
            gate(peer)
            send(r3.at[peer], r3s.at[peer], "sib>", ">sib" + mark, (i, sib))
    for d in ORDER:
        peer = (q + d) % 8
        send(rows16(r3, peer), r4.at[q], "vq>", ">vq", along_q(peer))
    r4[pl.ds(q, 1)] = r3[:, pl.ds(pl.multiple_of(q * 16, 16), 16), :].reshape(1, 8, 16, SIDE)

    for d in ORDER:
        peer = (z + d) % 8
        send(s3f.at[peer], r3f.at[z], "fz>", ">fz", along_z(peer))
    r3f[pl.ds(z, 1)] = s3f[pl.ds(z, 1)]

    for qq in range(8):
        g_all[0:SIDE, qq * SIDE : (qq + 1) * SIDE] = r3[:, qq * 16 : (qq + 1) * 16, :].reshape(SIDE, SIDE)
    arrived(tk.at[0:3], "tk>", ">tk2")
    own.wait()
    arrived(r3s.at[0:5], "sib>", ">sibc")
    arrived(r3s.at[0:3], "sib>", ">sibf")
    for qq in range(8):
        g_all[SIDE:, qq * SIDE : (qq + 1) * SIDE] = r3s[:, qq * 16 : (qq + 1) * 16, :].reshape(SIDE, SIDE)
    for t in range(4):
        sums = dot(g_all[...], tk[:, :, t * 256 : (t + 1) * 256].reshape(1024, 256)).reshape(2, 8, 2, 8, 256)
        to = core * 4 + t
        for s, who in enumerate((c, sib)):
            rows = [sums[s, :, f].reshape(64, 256) for f in range(2)]
            at = (2 * t + s) * 8
            part[at : at + 8] = jnp.concatenate(rows, axis=0).T.astype(BF16).reshape(8, 32, SIDE)

            def share(slot, at=at, to=to, who=who):
                peer = near(slot)
                send(part.at[at + peer], r5.at[z * 8 + q], "rs>", ">rs", (to * 8 + peer, who))

            if s == 1:
                share(0)
            else:

                @pl.when(to != z)
                def _(share=share):
                    share(0)

                @pl.when(to == z)
                def _(at=at):
                    pltpu.make_async_copy(part.at[at + q], r5.at[z * 8 + q], sem("self")).start()

            for slot in range(1, 8):
                share(slot)

    arrived(r4.at[0:7], "vq>", ">vq")
    for qq in range(8):
        x = r4[qq].astype(F32)
        vt[:, qq * 64 : (qq + 1) * 64] = x[:, :8].reshape(64, SIDE).T.astype(BF16)
        gt[:, qq * 64 : (qq + 1) * 64] = x[:, 8:].reshape(64, SIDE).T.astype(BF16)

    def columns(k):
        rows = pl.ds(pl.multiple_of(k * 512, 512), 512)
        over = (((1,), (1,)), ((), ()))
        a = lax.dot_general(vt[...], vw[rows, :], over, preferred_element_type=F32)
        return a + lax.dot_general(gt[...], gw[rows, :], over, preferred_element_type=F32)

    s7[0] = columns(2 * (1 - xh) + 1 - core)
    s7[1] = columns(2 * xh + 1 - core)
    send(s7, r7, "core>", ">core", (i, sib))
    far = columns(2 * (1 - xh) + core)
    here = columns(2 * xh + core)
    arrived(r7, "core>", ">core")
    s8[...] = (far + r7[0]).astype(BF16)
    send(s8, r8, "far>", ">far", (i, opp))
    here = here + r7[1]

    arrived(r3f.at[0:7], "fz>", ">fz")
    regroup(r3f, s4f)
    for d in ORDER:
        peer = (q + d) % 8
        send(s4f.at[peer], r4f.at[q], "fq>", ">fq", along_q(peer))
    r4f[pl.ds(q, 1)] = s4f[pl.ds(q, 1)]

    outs = [
        pltpu.make_async_copy(a, b, sem(f"out{t}"))
        for t, (a, b) in enumerate(zip((o_in, o_fil), (input_grad, filter_grad)))
    ]
    arrived(r8, "far>", ">far")
    o_in[...] = (here + r8[...].astype(F32)).astype(BF16)
    outs[0].start()
    arrived(r4f.at[0:7], "fq>", ">fq")
    for b in range(4):
        x = r4f[2 * b : 2 * b + 2].astype(F32).reshape(SIDE, SIDE)
        o_fil[:, b * SIDE : (b + 1) * SIDE] = x.T * SCALE
    outs[1].start()

    @pl.when(core == z // 4)
    def _():
        waiter(r5.at[0:63], "rs>", ">rs").wait()
        pltpu.make_async_copy(part.at[0], r5.at[0], sem("self")).wait()

    @pl.when(core != z // 4)
    def _():
        waiter(r5, "rs>", ">rs").wait()

    for size, out in (
        (r1_e.at[0:7], "ez>"), (r2_e.at[0:7], "eq>"), (r1_l.at[0:7], "lq>"), (r2_l.at[0:7], "lz>"),
        (r3.at[0:7], "vz>"), (r_c.at[0:7], "cq>"), (r3s, "sib>"), (r3f.at[0:7], "fz>"), (r4.at[0:7], "vq>"), (r4f.at[0:7], "fq>"),
        (tk.at[0:7], "tk>"), (r7, "core>"), (r8, "far>"),
    ):
        waiter(size, out, ">ez").wait_send()
    for copy in outs:
        copy.wait()


def local(tokens, value_weight, gate_weight, filters, cotangent):
    def v(*shape, dtype=BF16):
        return pltpu.VMEM(shape, dtype)

    whole = pl.BlockSpec(memory_space=pl.ANY)
    operands = [tokens, value_weight, gate_weight, filters, cotangent]
    operands += [jnp.asarray(t) for t in tables()]
    shape = jax.ShapeDtypeStruct
    input_grad, filter_grad = shape((128, 512), BF16), shape((128, 512), F32)
    weight_grad, terms = shape((32, 512), F32), shape((64, 32, 128), BF16)
    results = pl.pallas_call(
        kernel,
        out_shape=(input_grad, filter_grad, terms),
        in_specs=[whole] * 9,
        out_specs=(whole,) * 3,
        scratch_shapes=[pltpu.VMEM(t.shape, t.dtype) for t in operands] + [
            v(128, 128), v(4, 256, 256), v(64, 384),
            v(8, 64, 128), v(8, 128, 128), v(8, 64, 128), v(8, 128, 128),
            v(8, 64, 128), v(8, 64, 128), v(8, 8, 16, 128),
            v(512, 128, dtype=F32), v(1024, 128, dtype=F32), v(1024, 128, dtype=F32), v(512, 128, dtype=F32),
            v(8, 64, 128), v(8, 64, 128), v(8, 64, 128, dtype=F32),
            v(3, 512, 256, dtype=F32), v(2, 512, 256), v(512, 256, dtype=F32),
            v(8, 128, 128), v(8, 128, 128), v(8, 128, 128), v(8, 8, 16, 128),
            v(8, 64, 128), v(8, 64, 128), v(8, 64, 128), v(8, 64, 128),
            v(8, 128, 1024), v(256, 1024), v(64, 32, 128),
            v(128, 512), v(128, 512),
            v(2, 128, 512, dtype=F32), v(2, 128, 512, dtype=F32), v(128, 512), v(128, 512),
        ] + [pltpu.VMEM(t.shape, t.dtype) for t in (input_grad, filter_grad)] + [pltpu.SemaphoreType.DMA((len(SEMAPHORES),))],
        compiler_params=pltpu.CompilerParams(
            collective_id=0, has_side_effects=True, vmem_limit_bytes=60 * 1024 * 1024
        ),
        cost_estimate=pl.CostEstimate(flops=3_000_000_000, bytes_accessed=8_000_000, transcendentals=0),
    )(*operands)
    outputs = (input_grad, filter_grad, weight_grad, weight_grad)
    return pl.pallas_call(
        finish,
        out_shape=outputs,
        in_specs=[whole] * 3,
        out_specs=(whole,) * 4,
        scratch_shapes=[pltpu.VMEM(t.shape, t.dtype) for t in outputs + (terms,)] + [pltpu.SemaphoreType.DMA((7,))],
        compiler_params=pltpu.CompilerParams(vmem_limit_bytes=60 * 1024 * 1024),
    )(*results)


def finish(
    in_grad_in, filter_grad_in, terms_in, in_grad, filter_grad, vw_grad, gw_grad,
    o_in, o_fil, o_vw, o_gw, terms, sems,
):
    loads = [
        pltpu.make_async_copy(a, b, sems.at[t])
        for t, (a, b) in enumerate(((terms_in, terms), (in_grad_in, o_in), (filter_grad_in, o_fil)))
    ]
    for load in loads:
        load.start()
    stores = [
        pltpu.make_async_copy(a, b, sems.at[3 + t])
        for t, (a, b) in enumerate(((o_in, in_grad), (o_fil, filter_grad), (o_vw, vw_grad), (o_gw, gw_grad)))
    ]
    loads[0].wait()
    for qq in range(8):
        total = terms[qq].astype(F32)
        for zz in range(1, 8):
            total = total + terms[zz * 8 + qq].astype(F32)
        total = total * SCALE
        o_vw[:, qq * 64 : (qq + 1) * 64] = total[:, :64]
        o_gw[:, qq * 64 : (qq + 1) * 64] = total[:, 64:]
    stores[2].start()
    stores[3].start()
    for t in (1, 2):
        loads[t].wait()
        stores[t - 1].start()
    for store in stores:
        store.wait()


def solution(mesh):
    placed = (P("seq", None), P(None, "ch"), P(None, "ch"), P("seq", "ch"), P("seq", "ch"))
    return jax.shard_map(
        local,
        mesh=mesh,
        in_specs=placed,
        out_specs=(P("seq", "ch"),) * 4,
        check_vma=False,
    )
```

```python
import functools
import math

import jax
import jax.numpy as jnp
import ml_dtypes
import numpy as np
from jax import lax
from jax.experimental import pallas as pl
from jax.experimental.pallas import tpu as pltpu
from jax.sharding import PartitionSpec as P

MESH = pl.DeviceIdType.MESH
F32 = jnp.float32
BF16 = jnp.bfloat16
SIDE = 128
PADDED = SIDE * SIDE
SEQ = PADDED // 2
SCALE = SEQ**-0.5
ORDER = (4, 3, 5, 2, 6, 1, 7)
NEAR = ((0, 0), (1, 0), (0, 1), (0, 3), (1, 1), (1, 3), (0, 2), (1, 2))
BACK = (0, 1, 3, 2, 5, 4, 6, 7)
GROUPS = ((0, 1), (1, 4), (4, 8))
CLOSE, FAR = (2, 6, 1, 7), (4, 3, 5)
LOADS = ("fil", "cot", "tok", "vw", "gw", "first", "twist", "second", "last")
OUTGOING = ("ez", "eq", "lq", "lz", "cq", "vz", "sib", "fz", "vq", "fq", "tk", "rs", "core", "far")
INCOMING = (
    "ez", "eq", "lq1", "lq2", "lz0", "lz1", "lz2", "cq", "vzc", "vzf", "sibc", "sibf", "fz", "vq", "fq",
    "tk0", "tk1", "tk2", "rs", "core", "far",
)
SEMAPHORES = (
    tuple(t + ">" for t in OUTGOING)
    + tuple(">" + t for t in INCOMING)
    + ("own", "self", "out0", "out1")
    + LOADS
)


def split(table):
    high = table.astype(ml_dtypes.bfloat16)
    low = (table - high.astype(np.float64)).astype(ml_dtypes.bfloat16)
    return high, low


def tables():
    half = np.arange(64) + 0.5
    block = 2 * math.pi * np.outer(half, np.arange(64)) / SIDE
    first = np.concatenate([np.cos(block), -np.sin(block)], axis=0)
    first = np.concatenate(split(first), axis=1)
    twist = 2 * math.pi * np.outer(half, np.arange(SIDE)) / PADDED
    twist = np.concatenate([np.cos(twist), np.sin(twist)], axis=0).astype(np.float32)
    inner = 2 * math.pi * np.outer(np.arange(SIDE), np.arange(SIDE)) / SIDE
    c, s = np.cos(inner), np.sin(inner)
    forward = np.block([[c, -s], [s, c]])
    inverse = np.block([[c, s], [-s, c]])
    second = np.concatenate(split(forward) + split(inverse), axis=0)
    last = np.concatenate([np.cos(block.T), -np.sin(block.T)], axis=1) * (2.0 / PADDED)
    high, low = split(last)
    last = np.concatenate([high, high, low], axis=1)
    return tuple(t.astype(np.float32) for t in (first, twist, second, last))


def dot(a, b):
    return jnp.dot(a, b, preferred_element_type=F32)


def halves(x):
    high = x.astype(BF16)
    return high, (x - high.astype(F32)).astype(BF16)


def kernel(
    tok_in, vw_in, gw_in, fil_in, cot_in, t_first_in, t_twist_in, t_second_in, t_last_in,
    input_grad, filter_grad, r5,
    tok, vw, gw, fil, cot, t_first, t_twist, t_second, t_last,
    t_first16, t_second16, t_last16, s_e, s_l, r1_e, r1_l, s2_e, r2_e, r2_l, u_e, u_l, w_vg, w_f,
    s_c, r_c, wide_c,
    spec, lhs, mid, s3, r3, r3s, r4, s3f, r3f, s4f, r4f,
    tk, g_all, part, vt, gt, s7, r7, s8, r8, o_in, o_fil, sems,
):
    i = lax.axis_index("seq")
    c = lax.axis_index("ch")
    z, q = i // 8, i % 8
    core, xh = c % 2, c // 2
    sib = c + 1 - 2 * core
    opp = (c + 2) % 4

    def along_z(zz):
        return (zz * 8 + q, c)

    def along_q(qq):
        return (z * 8 + qq, c)

    def near(slot):
        dx, dy = NEAR[slot]
        return (q // 4 + dx) % 2 * 4 + (q + dy) % 4

    def sem(name):
        return sems.at[SEMAPHORES.index(name)]

    loads = {}
    sources = (fil_in, cot_in, tok_in, vw_in, gw_in, t_first_in, t_twist_in, t_second_in, t_last_in)
    places = (fil, cot, tok, vw, gw, t_first, t_twist, t_second, t_last)
    for name, src, dst in zip(LOADS, sources, places):
        loads[name] = pltpu.make_async_copy(src, dst, sem(name))
        loads[name].start()

    barrier = pltpu.get_barrier_semaphore()
    peers = 0
    for d in range(1, 8):
        for who in (along_z((z + d) % 8), along_q((q + d) % 8)):
            pl.semaphore_signal(barrier, inc=1, device_id=who, device_id_type=MESH)
            peers += 1
    for who in ((i, sib), (i, opp), (along_q(near(1))[0], opp)):
        pl.semaphore_signal(barrier, inc=1, device_id=who, device_id_type=MESH)
        peers += 1

    def pair(a, b):
        a = a.T.reshape(16, 8, SIDE)
        b = b.T.reshape(16, 8, SIDE)
        return jnp.concatenate([a, b], axis=1).astype(BF16).reshape(2, SIDE, SIDE)

    def send(src, dst, out, into, who):
        pltpu.make_async_remote_copy(
            src_ref=src, dst_ref=dst, send_sem=sem(out), recv_sem=sem(into), device_id=who, device_id_type=MESH
        ).start()

    def waiter(size, out, into):
        return pltpu.make_async_remote_copy(
            src_ref=size, dst_ref=size, send_sem=sem(out), recv_sem=sem(into),
            device_id=(i, sib), device_id_type=MESH,
        )

    def arrived(size, out, into):
        waiter(size, out, into).wait_recv()

    def rows16(ref, at):
        return ref.at[:, pl.ds(pl.multiple_of(at * 16, 16), 16), :]

    loads["fil"].wait()
    for b in range(4):
        rows = fil[:, b * SIDE : (b + 1) * SIDE].T.reshape(2, 8, 8, SIDE)
        for zz in range(8):
            s_e[zz, b * 16 : (b + 1) * 16] = rows[:, zz].reshape(16, SIDE).astype(BF16)
    loads["tok"].wait()
    own_cols = pl.ds(pl.multiple_of(core * 1024, 1024), 1024)
    half = tok.at[:, own_cols]
    own = pltpu.make_async_copy(half, tk.at[q], sem("own"))
    own.start()

    def give(src, dst, at, who):
        send(src, dst, "tk>", f">tk{at}", who)

    up_half, down_half = slice(0, 64), slice(64, SIDE)
    ahead, behind = along_q(near(2)), along_q(near(3))
    beside, across = along_q(near(1)), (along_q(near(1))[0], opp)

    def sideways(block):
        give(tk.at[block, up_half], tk.at[block, up_half], 2, beside)
        give(tk.at[block, down_half], tk.at[block, down_half], 2, across)

    def pieces(first, last):
        for k in range(first, last):
            rows = slice(16 * k, 16 * (k + 1))
            for who in (ahead, behind, beside if k < 4 else across):
                give(tok.at[rows, own_cols], tk.at[q, rows], 0, who)

    pl.semaphore_wait(barrier, peers)
    for d in ORDER:
        peer = (z + d) % 8
        send(s_e.at[peer], r1_e.at[z], "ez>", ">ez", along_z(peer))
    r1_e[pl.ds(z, 1)] = s_e[pl.ds(z, 1)]

    pieces(0, 2)
    loads["cot"].wait()
    loads["vw"].wait()
    loads["gw"].wait()
    for b in range(2):
        lanes = slice(b * 256, (b + 1) * 256)
        val = dot(tok[...], vw[:, lanes])
        up = dot(tok[...], gw[:, lanes]) * cot[:, lanes].astype(F32)
        for e in range(2):
            part_lanes = slice(e * SIDE, (e + 1) * SIDE)
            at = 4 * b + 2 * e
            s_l[at : at + 2] = pair(val[:, part_lanes], up[:, part_lanes])
    for group in (1, 2):
        for slot in range(*GROUPS[group]):
            send(s_l.at[near(slot)], r1_l.at[BACK[slot]], "lq>", f">lq{group}", along_q(near(slot)))
    r1_l[0] = s_l[pl.ds(q, 1)].reshape(SIDE, SIDE)

    pieces(2, 4)
    def onward(group):
        a, b = GROUPS[group]
        if group:
            arrived(r1_l.at[a:b], "lq>", f">lq{group}")
        for d in ORDER:
            peer = (z + d) % 8
            rows = pl.ds(pl.multiple_of(peer * 16, 16), 16)
            send(r1_l.at[a:b, rows, :], r2_l.at[z, a:b], "lz>", f">lz{group}", along_z(peer))
        mine = r1_l[a:b, pl.ds(pl.multiple_of(z * 16, 16), 16), :]
        r2_l[pl.ds(z, 1), a:b] = mine.reshape(1, b - a, 16, SIDE)

    onward(0)
    for name in ("first", "twist", "second", "last"):
        loads[name].wait()
    cw = t_twist[0:64]
    sw = t_twist[64:128]
    for t in range(4):
        t_second16[t] = t_second[256 * t : 256 * (t + 1)].astype(BF16)
    t_first16[...] = t_first[...].astype(BF16)
    t_last16[...] = t_last[...].astype(BF16)
    g_high, g_low, i_high, i_low = (t_second16[t] for t in range(4))
    for b in range(4):
        lanes = slice(b * SIDE, (b + 1) * SIDE)
        s_c[2 * b : 2 * b + 2] = cot[:, lanes].astype(F32).T.astype(BF16).reshape(2, 64, SIDE)
    onward(1)
    pieces(4, 5)
    def regroup(src, dst):
        x = src[...].astype(F32).reshape(8, 8, 8, SIDE)
        for qq in range(8):
            dst[qq] = x[:, qq].reshape(64, SIDE).astype(BF16)

    arrived(r1_e.at[0:7], "ez>", ">ez")
    regroup(r1_e, s2_e)
    for d in ORDER:
        peer = (q + d) % 8
        send(s2_e.at[peer], r2_e.at[q], "eq>", ">eq", along_q(peer))
    r2_e[pl.ds(q, 1)] = s2_e[pl.ds(q, 1)]
    onward(2)

    pieces(5, 6)
    pieces(6, 8)
    for d in ORDER:
        peer = (q + d) % 8
        send(s_c.at[peer], r_c.at[q], "cq>", ">cq", along_q(peer))
    r_c[pl.ds(q, 1)] = s_c[pl.ds(q, 1)]

    def put(at, x):
        high, low = halves(x)
        lhs[0, at * 64 : (at + 1) * 64] = high
        lhs[1, at * 64 : (at + 1) * 64] = low

    def forward(u, base, stride, out):
        for r in range(0, 8, 2):
            x = [u[pl.ds(base + r + e, 64, stride=stride), :] for e in range(2)]
            x = jnp.concatenate(x, axis=1).astype(BF16)
            a = dot(t_first16[...], jnp.concatenate([x, x], axis=0))
            for e in range(2):
                re = a[:64, e * SIDE : (e + 1) * SIDE]
                im = a[64:, e * SIDE : (e + 1) * SIDE]
                put(r + e, jnp.concatenate([re * cw + im * sw, im * cw - re * sw], axis=1))
        spec[out] = dot(lhs[0], g_high) + (dot(lhs[1], g_high) + dot(lhs[0], g_low))

    def inverse(left, right, conjugate, store):
        for r in range(8):
            rows = slice(r * 64, (r + 1) * 64)
            ar, ai = spec[left, rows, :SIDE], spec[left, rows, SIDE:]
            br, bi = spec[right, rows, :SIDE], spec[right, rows, SIDE:]
            if conjugate:
                p = [ar * br + ai * bi, ar * bi - ai * br]
            else:
                p = [ar * br - ai * bi, ar * bi + ai * br]
            put(r, jnp.concatenate(p, axis=1))
        mid[...] = dot(lhs[0], i_high) + (dot(lhs[1], i_high) + dot(lhs[0], i_low))
        for r in range(0, 8, 2):
            cols = []
            for e in range(2):
                rows = slice((r + e) * 64, (r + e + 1) * 64)
                re, im = mid[rows, :SIDE], mid[rows, SIDE:]
                cols.append(jnp.concatenate([re * cw - im * sw, im * cw + re * sw], axis=0))
            high, low = halves(jnp.concatenate(cols, axis=1))
            y = dot(t_last16[...], jnp.concatenate([high, low, high], axis=0))
            for e in range(2):
                store(r + e, y[:, e * SIDE : (e + 1) * SIDE])

    arrived(r2_e.at[0:7], "eq>", ">eq")
    for qq in range(8):
        x = r2_e[qq].astype(F32)
        for zz in range(8):
            u_e[zz * 64 + qq * 8 : zz * 64 + qq * 8 + 8] = x[zz * 8 : zz * 8 + 8]
    forward(u_e, 0, 8, 0)
    for group, (a, b) in enumerate(GROUPS):
        arrived(r2_l.at[0:7, a:b], "lz>", f">lz{group}")
        for slot in range(a, b):
            for zz in range(8):
                at = pl.multiple_of(zz * SIDE + near(slot) * 16, 16)
                u_l[pl.ds(at, 16), :] = r2_l[zz, slot].astype(F32)
    arrived(tk.at[0:3], "tk>", ">tk0")
    give(tk.at[near(2), up_half], tk.at[near(2), up_half], 1, behind)
    give(tk.at[near(3), down_half], tk.at[near(3), down_half], 1, ahead)
    sideways(near(2))
    sideways(near(3))
    forward(u_l, 8, 16, 2)
    forward(u_l, 0, 16, 1)

    def store_v(r, y):
        w_vg[pl.ds(r, 64, stride=16), :] = y

    def store_g(r, y):
        w_vg[pl.ds(8 + r, 64, stride=16), :] = y

    def store_f(r, y):
        w_f[pl.ds(r, 64, stride=8), :] = y

    inverse(0, 2, True, store_v)
    inverse(0, 1, False, store_g)
    for zz in range(8):
        s3[zz] = w_vg[zz * SIDE : (zz + 1) * SIDE].astype(BF16)
    for ds, mark in ((FAR, "f"), (CLOSE, "c")):
        for d in ds:
            peer = (z + d) % 8
            send(s3.at[peer], r3.at[z], "vz>", ">vz" + mark, along_z(peer))
    r3[pl.ds(z, 1)] = s3[pl.ds(z, 1)]
    inverse(1, 2, True, store_f)
    for zz in range(8):
        s3f[zz] = w_f[zz * 64 : (zz + 1) * 64].astype(BF16)

    arrived(tk.at[0], "tk>", ">tk1")
    sideways(near(6))
    arrived(r_c.at[0:7], "cq>", ">cq")
    wide_c[...] = r_c[...].astype(F32)

    def gate(at):
        x = r3[pl.ds(at, 1)].astype(F32).reshape(8, 16, SIDE)
        factor = wide_c[:, pl.ds(pl.multiple_of(at * 8, 8), 8), :]
        x = jnp.concatenate([x[:, :8], x[:, 8:] * factor], axis=1)
        r3[pl.ds(at, 1)] = x.astype(BF16).reshape(1, SIDE, SIDE)

    gate(z)
    send(r3.at[z], r3s.at[z], "sib>", ">sibc", (i, sib))
    for ds, mark in ((CLOSE, "c"), (FAR, "f")):
        arrived(r3.at[0 : len(ds)], "vz>", ">vz" + mark)
        for d in ds:
            peer = (z + d) % 8
            gate(peer)
            send(r3.at[peer], r3s.at[peer], "sib>", ">sib" + mark, (i, sib))
    for d in ORDER:
        peer = (q + d) % 8
        send(rows16(r3, peer), r4.at[q], "vq>", ">vq", along_q(peer))
    r4[pl.ds(q, 1)] = r3[:, pl.ds(pl.multiple_of(q * 16, 16), 16), :].reshape(1, 8, 16, SIDE)

    for d in ORDER:
        peer = (z + d) % 8
        send(s3f.at[peer], r3f.at[z], "fz>", ">fz", along_z(peer))
    r3f[pl.ds(z, 1)] = s3f[pl.ds(z, 1)]

    for qq in range(8):
        g_all[0:SIDE, qq * SIDE : (qq + 1) * SIDE] = r3[:, qq * 16 : (qq + 1) * 16, :].reshape(SIDE, SIDE)
    arrived(tk.at[0:3], "tk>", ">tk2")
    own.wait()
    arrived(r3s.at[0:5], "sib>", ">sibc")
    arrived(r3s.at[0:3], "sib>", ">sibf")
    for qq in range(8):
        g_all[SIDE:, qq * SIDE : (qq + 1) * SIDE] = r3s[:, qq * 16 : (qq + 1) * 16, :].reshape(SIDE, SIDE)
    for t in range(4):
        sums = dot(g_all[...], tk[:, :, t * 256 : (t + 1) * 256].reshape(1024, 256)).reshape(2, 8, 2, 8, 256)
        to = core * 4 + t
        for s, who in enumerate((c, sib)):
            rows = [sums[s, :, f].reshape(64, 256) for f in range(2)]
            at = (2 * t + s) * 8
            part[at : at + 8] = jnp.concatenate(rows, axis=0).T.astype(BF16).reshape(8, 32, SIDE)

            def share(slot, at=at, to=to, who=who):
                peer = near(slot)
                send(part.at[at + peer], r5.at[z * 8 + q], "rs>", ">rs", (to * 8 + peer, who))

            if s == 1:
                share(0)
            else:

                @pl.when(to != z)
                def _(share=share):
                    share(0)

                @pl.when(to == z)
                def _(at=at):
                    pltpu.make_async_copy(part.at[at + q], r5.at[z * 8 + q], sem("self")).start()

            for slot in range(1, 8):
                share(slot)

    arrived(r4.at[0:7], "vq>", ">vq")
    for qq in range(8):
        x = r4[qq].astype(F32)
        vt[:, qq * 64 : (qq + 1) * 64] = x[:, :8].reshape(64, SIDE).T.astype(BF16)
        gt[:, qq * 64 : (qq + 1) * 64] = x[:, 8:].reshape(64, SIDE).T.astype(BF16)

    def columns(k):
        rows = pl.ds(pl.multiple_of(k * 512, 512), 512)
        over = (((1,), (1,)), ((), ()))
        a = lax.dot_general(vt[...], vw[rows, :], over, preferred_element_type=F32)
        return a + lax.dot_general(gt[...], gw[rows, :], over, preferred_element_type=F32)

    s7[0] = columns(2 * (1 - xh) + 1 - core)
    s7[1] = columns(2 * xh + 1 - core)
    send(s7, r7, "core>", ">core", (i, sib))
    far = columns(2 * (1 - xh) + core)
    here = columns(2 * xh + core)
    arrived(r7, "core>", ">core")
    s8[...] = (far + r7[0]).astype(BF16)
    send(s8, r8, "far>", ">far", (i, opp))
    here = here + r7[1]

    arrived(r3f.at[0:7], "fz>", ">fz")
    regroup(r3f, s4f)
    for d in ORDER:
        peer = (q + d) % 8
        send(s4f.at[peer], r4f.at[q], "fq>", ">fq", along_q(peer))
    r4f[pl.ds(q, 1)] = s4f[pl.ds(q, 1)]

    outs = [
        pltpu.make_async_copy(a, b, sem(f"out{t}"))
        for t, (a, b) in enumerate(zip((o_in, o_fil), (input_grad, filter_grad)))
    ]
    arrived(r8, "far>", ">far")
    o_in[...] = (here + r8[...].astype(F32)).astype(BF16)
    outs[0].start()
    arrived(r4f.at[0:7], "fq>", ">fq")
    for b in range(4):
        x = r4f[2 * b : 2 * b + 2].astype(F32).reshape(SIDE, SIDE)
        o_fil[:, b * SIDE : (b + 1) * SIDE] = x.T * SCALE
    outs[1].start()

    @pl.when(core == z // 4)
    def _():
        waiter(r5.at[0:63], "rs>", ">rs").wait()
        pltpu.make_async_copy(part.at[0], r5.at[0], sem("self")).wait()

    @pl.when(core != z // 4)
    def _():
        waiter(r5, "rs>", ">rs").wait()

    for size, out in (
        (r1_e.at[0:7], "ez>"), (r2_e.at[0:7], "eq>"), (r1_l.at[0:7], "lq>"), (r2_l.at[0:7], "lz>"),
        (r3.at[0:7], "vz>"), (r_c.at[0:7], "cq>"), (r3s, "sib>"), (r3f.at[0:7], "fz>"), (r4.at[0:7], "vq>"), (r4f.at[0:7], "fq>"),
        (tk.at[0:7], "tk>"), (r7, "core>"), (r8, "far>"),
    ):
        waiter(size, out, ">ez").wait_send()
    for copy in outs:
        copy.wait()


def local(tokens, value_weight, gate_weight, filters, cotangent):
    def v(*shape, dtype=BF16):
        return pltpu.VMEM(shape, dtype)

    whole = pl.BlockSpec(memory_space=pl.ANY)
    operands = [tokens, value_weight, gate_weight, filters, cotangent]
    operands += [jnp.asarray(t) for t in tables()]
    shape = jax.ShapeDtypeStruct
    input_grad, filter_grad = shape((128, 512), BF16), shape((128, 512), F32)
    weight_grad, terms = shape((32, 512), F32), shape((64, 32, 128), BF16)
    results = pl.pallas_call(
        kernel,
        out_shape=(input_grad, filter_grad, terms),
        in_specs=[whole] * 9,
        out_specs=(whole,) * 3,
        scratch_shapes=[pltpu.VMEM(t.shape, t.dtype) for t in operands] + [
            v(128, 128), v(4, 256, 256), v(64, 384),
            v(8, 64, 128), v(8, 128, 128), v(8, 64, 128), v(8, 128, 128),
            v(8, 64, 128), v(8, 64, 128), v(8, 8, 16, 128),
            v(512, 128, dtype=F32), v(1024, 128, dtype=F32), v(1024, 128, dtype=F32), v(512, 128, dtype=F32),
            v(8, 64, 128), v(8, 64, 128), v(8, 64, 128, dtype=F32),
            v(3, 512, 256, dtype=F32), v(2, 512, 256), v(512, 256, dtype=F32),
            v(8, 128, 128), v(8, 128, 128), v(8, 128, 128), v(8, 8, 16, 128),
            v(8, 64, 128), v(8, 64, 128), v(8, 64, 128), v(8, 64, 128),
            v(8, 128, 1024), v(256, 1024), v(64, 32, 128),
            v(128, 512), v(128, 512),
            v(2, 128, 512, dtype=F32), v(2, 128, 512, dtype=F32), v(128, 512), v(128, 512),
        ] + [pltpu.VMEM(t.shape, t.dtype) for t in (input_grad, filter_grad)] + [pltpu.SemaphoreType.DMA((len(SEMAPHORES),))],
        compiler_params=pltpu.CompilerParams(
            collective_id=0, has_side_effects=True, vmem_limit_bytes=60 * 1024 * 1024
        ),
        cost_estimate=pl.CostEstimate(flops=3_000_000_000, bytes_accessed=8_000_000, transcendentals=0),
    )(*operands)
    outputs = (input_grad, filter_grad, weight_grad, weight_grad)
    return pl.pallas_call(
        finish,
        out_shape=outputs,
        in_specs=[whole] * 3,
        out_specs=(whole,) * 4,
        scratch_shapes=[pltpu.VMEM(t.shape, t.dtype) for t in outputs + (terms,)] + [pltpu.SemaphoreType.DMA((7,))],
        compiler_params=pltpu.CompilerParams(vmem_limit_bytes=60 * 1024 * 1024),
    )(*results)


def finish(
    in_grad_in, filter_grad_in, terms_in, in_grad, filter_grad, vw_grad, gw_grad,
    o_in, o_fil, o_vw, o_gw, terms, sems,
):
    loads = [
        pltpu.make_async_copy(a, b, sems.at[t])
        for t, (a, b) in enumerate(((terms_in, terms), (in_grad_in, o_in), (filter_grad_in, o_fil)))
    ]
    for load in loads:
        load.start()
    stores = [
        pltpu.make_async_copy(a, b, sems.at[3 + t])
        for t, (a, b) in enumerate(((o_in, in_grad), (o_fil, filter_grad), (o_vw, vw_grad), (o_gw, gw_grad)))
    ]
    loads[0].wait()
    for qq in range(8):
        total = terms[qq].astype(F32)
        for zz in range(1, 8):
            total = total + terms[zz * 8 + qq].astype(F32)
        total = total * SCALE
        o_vw[:, qq * 64 : (qq + 1) * 64] = total[:, :64]
        o_gw[:, qq * 64 : (qq + 1) * 64] = total[:, 64:]
    stores[2].start()
    stores[3].start()
    for t in (1, 2):
        loads[t].wait()
        stores[t - 1].start()
    for store in stores:
        store.wait()


def solution(mesh):
    placed = (P("seq", None), P(None, "ch"), P(None, "ch"), P("seq", "ch"), P("seq", "ch"))
    return jax.shard_map(
        local,
        mesh=mesh,
        in_specs=placed,
        out_specs=(P("seq", "ch"),) * 4,
        check_vma=False,
    )
```

```python
import functools
import math

import jax
import jax.numpy as jnp
import ml_dtypes
import numpy as np
from jax import lax
from jax.experimental import pallas as pl
from jax.experimental.pallas import tpu as pltpu
from jax.sharding import PartitionSpec as P

MESH = pl.DeviceIdType.MESH
F32 = jnp.float32
BF16 = jnp.bfloat16
SIDE = 128
PADDED = SIDE * SIDE
SEQ = PADDED // 2
SCALE = SEQ**-0.5
ORDER = (4, 3, 5, 2, 6, 1, 7)
NEAR = ((0, 0), (1, 0), (0, 1), (0, 3), (1, 1), (1, 3), (0, 2), (1, 2))
BACK = (0, 1, 3, 2, 5, 4, 6, 7)
GROUPS = ((0, 1), (1, 4), (4, 8))
CLOSE, FAR = (2, 6, 1, 7), (4, 3, 5)
LOADS = ("fil", "cot", "tok", "vw", "gw", "first", "twist", "second", "last")
OUTGOING = ("ez", "eq", "lq", "lz", "cq", "vz", "sib", "fz", "vq", "fq", "tk", "rs", "core", "far")
INCOMING = (
    "ez", "eq", "lq1", "lq2", "lz0", "lz1", "lz2", "cq", "vzc", "vzf", "sibc", "sibf", "fz", "vq", "fq",
    "tk0", "tk1", "tk2", "rs", "core", "far",
)
SEMAPHORES = (
    tuple(t + ">" for t in OUTGOING)
    + tuple(">" + t for t in INCOMING)
    + ("own", "self", "out0", "out1")
    + LOADS
)


def split(table):
    high = table.astype(ml_dtypes.bfloat16)
    low = (table - high.astype(np.float64)).astype(ml_dtypes.bfloat16)
    return high, low


def tables():
    half = np.arange(64) + 0.5
    block = 2 * math.pi * np.outer(half, np.arange(64)) / SIDE
    first = np.concatenate([np.cos(block), -np.sin(block)], axis=0)
    first = np.concatenate(split(first), axis=1)
    twist = 2 * math.pi * np.outer(half, np.arange(SIDE)) / PADDED
    twist = np.concatenate([np.cos(twist), np.sin(twist)], axis=0).astype(np.float32)
    inner = 2 * math.pi * np.outer(np.arange(SIDE), np.arange(SIDE)) / SIDE
    c, s = np.cos(inner), np.sin(inner)
    forward = np.block([[c, -s], [s, c]])
    inverse = np.block([[c, s], [-s, c]])
    second = np.concatenate(split(forward) + split(inverse), axis=0)
    last = np.concatenate([np.cos(block.T), -np.sin(block.T)], axis=1) * (2.0 / PADDED)
    high, low = split(last)
    last = np.concatenate([high, high, low], axis=1)
    return tuple(t.astype(np.float32) for t in (first, twist, second, last))


def dot(a, b):
    return jnp.dot(a, b, preferred_element_type=F32)


def halves(x):
    high = x.astype(BF16)
    return high, (x - high.astype(F32)).astype(BF16)


def kernel(
    tok_in, vw_in, gw_in, fil_in, cot_in, t_first_in, t_twist_in, t_second_in, t_last_in,
    input_grad, filter_grad, r5,
    tok, vw, gw, fil, cot, t_first, t_twist, t_second, t_last,
    t_first16, t_second16, t_last16, s_e, s_l, r1_e, r1_l, s2_e, r2_e, r2_l, u_e, u_l, w_vg, w_f,
    s_c, r_c, wide_c,
    spec, lhs, mid, s3, r3, r3s, r4, s3f, r3f, s4f, r4f,
    tk, g_all, part, vt, gt, s7, r7, s8, r8, o_in, o_fil, sems,
):
    i = lax.axis_index("seq")
    c = lax.axis_index("ch")
    z, q = i // 8, i % 8
    core, xh = c % 2, c // 2
    sib = c + 1 - 2 * core
    opp = (c + 2) % 4

    def along_z(zz):
        return (zz * 8 + q, c)

    def along_q(qq):
        return (z * 8 + qq, c)

    def near(slot):
        dx, dy = NEAR[slot]
        return (q // 4 + dx) % 2 * 4 + (q + dy) % 4

    def sem(name):
        return sems.at[SEMAPHORES.index(name)]

    loads = {}
    sources = (fil_in, cot_in, tok_in, vw_in, gw_in, t_first_in, t_twist_in, t_second_in, t_last_in)
    places = (fil, cot, tok, vw, gw, t_first, t_twist, t_second, t_last)
    for name, src, dst in zip(LOADS, sources, places):
        loads[name] = pltpu.make_async_copy(src, dst, sem(name))
        loads[name].start()

    barrier = pltpu.get_barrier_semaphore()
    peers = 0
    for d in range(1, 8):
        for who in (along_z((z + d) % 8), along_q((q + d) % 8)):
            pl.semaphore_signal(barrier, inc=1, device_id=who, device_id_type=MESH)
            peers += 1
    for who in ((i, sib), (i, opp), (along_q(near(1))[0], opp)):
        pl.semaphore_signal(barrier, inc=1, device_id=who, device_id_type=MESH)
        peers += 1

    def pair(a, b):
        a = a.T.reshape(16, 8, SIDE)
        b = b.T.reshape(16, 8, SIDE)
        return jnp.concatenate([a, b], axis=1).astype(BF16).reshape(2, SIDE, SIDE)

    def send(src, dst, out, into, who):
        pltpu.make_async_remote_copy(
            src_ref=src, dst_ref=dst, send_sem=sem(out), recv_sem=sem(into), device_id=who, device_id_type=MESH
        ).start()

    def waiter(size, out, into):
        return pltpu.make_async_remote_copy(
            src_ref=size, dst_ref=size, send_sem=sem(out), recv_sem=sem(into),
            device_id=(i, sib), device_id_type=MESH,
        )

    def arrived(size, out, into):
        waiter(size, out, into).wait_recv()

    def rows16(ref, at):
        return ref.at[:, pl.ds(pl.multiple_of(at * 16, 16), 16), :]

    loads["fil"].wait()
    for b in range(4):
        rows = fil[:, b * SIDE : (b + 1) * SIDE].T.reshape(2, 8, 8, SIDE)
        for zz in range(8):
            s_e[zz, b * 16 : (b + 1) * 16] = rows[:, zz].reshape(16, SIDE).astype(BF16)
    loads["tok"].wait()
    own_cols = pl.ds(pl.multiple_of(core * 1024, 1024), 1024)
    half = tok.at[:, own_cols]
    own = pltpu.make_async_copy(half, tk.at[q], sem("own"))
    own.start()

    def give(src, dst, at, who):
        send(src, dst, "tk>", f">tk{at}", who)

    up_half, down_half = slice(0, 64), slice(64, SIDE)
    ahead, behind = along_q(near(2)), along_q(near(3))
    beside, across = along_q(near(1)), (along_q(near(1))[0], opp)

    def sideways(block):
        give(tk.at[block, up_half], tk.at[block, up_half], 2, beside)
        give(tk.at[block, down_half], tk.at[block, down_half], 2, across)

    def pieces(first, last):
        for k in range(first, last):
            rows = slice(16 * k, 16 * (k + 1))
            for who in (ahead, behind, beside if k < 4 else across):
                give(tok.at[rows, own_cols], tk.at[q, rows], 0, who)

    pl.semaphore_wait(barrier, peers)
    for d in ORDER:
        peer = (z + d) % 8
        send(s_e.at[peer], r1_e.at[z], "ez>", ">ez", along_z(peer))
    r1_e[pl.ds(z, 1)] = s_e[pl.ds(z, 1)]

    pieces(0, 3)
    loads["cot"].wait()
    loads["vw"].wait()
    loads["gw"].wait()
    for b in range(2):
        lanes = slice(b * 256, (b + 1) * 256)
        val = dot(tok[...], vw[:, lanes])
        up = dot(tok[...], gw[:, lanes]) * cot[:, lanes].astype(F32)
        for e in range(2):
            part_lanes = slice(e * SIDE, (e + 1) * SIDE)
            at = 4 * b + 2 * e
            s_l[at : at + 2] = pair(val[:, part_lanes], up[:, part_lanes])
    for group in (1, 2):
        for slot in range(*GROUPS[group]):
            send(s_l.at[near(slot)], r1_l.at[BACK[slot]], "lq>", f">lq{group}", along_q(near(slot)))
    r1_l[0] = s_l[pl.ds(q, 1)].reshape(SIDE, SIDE)

    pieces(3, 5)
    def onward(group):
        a, b = GROUPS[group]
        if group:
            arrived(r1_l.at[a:b], "lq>", f">lq{group}")
        for d in ORDER:
            peer = (z + d) % 8
            rows = pl.ds(pl.multiple_of(peer * 16, 16), 16)
            send(r1_l.at[a:b, rows, :], r2_l.at[z, a:b], "lz>", f">lz{group}", along_z(peer))
        mine = r1_l[a:b, pl.ds(pl.multiple_of(z * 16, 16), 16), :]
        r2_l[pl.ds(z, 1), a:b] = mine.reshape(1, b - a, 16, SIDE)

    onward(0)
    for name in ("first", "twist", "second", "last"):
        loads[name].wait()
    cw = t_twist[0:64]
    sw = t_twist[64:128]
    for t in range(4):
        t_second16[t] = t_second[256 * t : 256 * (t + 1)].astype(BF16)
    t_first16[...] = t_first[...].astype(BF16)
    t_last16[...] = t_last[...].astype(BF16)
    g_high, g_low, i_high, i_low = (t_second16[t] for t in range(4))
    for b in range(4):
        lanes = slice(b * SIDE, (b + 1) * SIDE)
        s_c[2 * b : 2 * b + 2] = cot[:, lanes].astype(F32).T.astype(BF16).reshape(2, 64, SIDE)
    onward(1)
    pieces(5, 6)
    def regroup(src, dst):
        x = src[...].astype(F32).reshape(8, 8, 8, SIDE)
        for qq in range(8):
            dst[qq] = x[:, qq].reshape(64, SIDE).astype(BF16)

    arrived(r1_e.at[0:7], "ez>", ">ez")
    regroup(r1_e, s2_e)
    for d in ORDER:
        peer = (q + d) % 8
        send(s2_e.at[peer], r2_e.at[q], "eq>", ">eq", along_q(peer))
    r2_e[pl.ds(q, 1)] = s2_e[pl.ds(q, 1)]
    onward(2)

    pieces(6, 7)
    pieces(7, 8)
    for d in ORDER:
        peer = (q + d) % 8
        send(s_c.at[peer], r_c.at[q], "cq>", ">cq", along_q(peer))
    r_c[pl.ds(q, 1)] = s_c[pl.ds(q, 1)]

    def put(at, x):
        high, low = halves(x)
        lhs[0, at * 64 : (at + 1) * 64] = high
        lhs[1, at * 64 : (at + 1) * 64] = low

    def forward(u, base, stride, out):
        for r in range(0, 8, 2):
            x = [u[pl.ds(base + r + e, 64, stride=stride), :] for e in range(2)]
            x = jnp.concatenate(x, axis=1).astype(BF16)
            a = dot(t_first16[...], jnp.concatenate([x, x], axis=0))
            for e in range(2):
                re = a[:64, e * SIDE : (e + 1) * SIDE]
                im = a[64:, e * SIDE : (e + 1) * SIDE]
                put(r + e, jnp.concatenate([re * cw + im * sw, im * cw - re * sw], axis=1))
        spec[out] = dot(lhs[0], g_high) + (dot(lhs[1], g_high) + dot(lhs[0], g_low))

    def inverse(left, right, conjugate, store):
        for r in range(8):
            rows = slice(r * 64, (r + 1) * 64)
            ar, ai = spec[left, rows, :SIDE], spec[left, rows, SIDE:]
            br, bi = spec[right, rows, :SIDE], spec[right, rows, SIDE:]
            if conjugate:
                p = [ar * br + ai * bi, ar * bi - ai * br]
            else:
                p = [ar * br - ai * bi, ar * bi + ai * br]
            put(r, jnp.concatenate(p, axis=1))
        mid[...] = dot(lhs[0], i_high) + (dot(lhs[1], i_high) + dot(lhs[0], i_low))
        for r in range(0, 8, 2):
            cols = []
            for e in range(2):
                rows = slice((r + e) * 64, (r + e + 1) * 64)
                re, im = mid[rows, :SIDE], mid[rows, SIDE:]
                cols.append(jnp.concatenate([re * cw - im * sw, im * cw + re * sw], axis=0))
            high, low = halves(jnp.concatenate(cols, axis=1))
            y = dot(t_last16[...], jnp.concatenate([high, low, high], axis=0))
            for e in range(2):
                store(r + e, y[:, e * SIDE : (e + 1) * SIDE])

    arrived(r2_e.at[0:7], "eq>", ">eq")
    for qq in range(8):
        x = r2_e[qq].astype(F32)
        for zz in range(8):
            u_e[zz * 64 + qq * 8 : zz * 64 + qq * 8 + 8] = x[zz * 8 : zz * 8 + 8]
    forward(u_e, 0, 8, 0)
    for group, (a, b) in enumerate(GROUPS):
        arrived(r2_l.at[0:7, a:b], "lz>", f">lz{group}")
        for slot in range(a, b):
            for zz in range(8):
                at = pl.multiple_of(zz * SIDE + near(slot) * 16, 16)
                u_l[pl.ds(at, 16), :] = r2_l[zz, slot].astype(F32)
    arrived(tk.at[0:3], "tk>", ">tk0")
    give(tk.at[near(2), up_half], tk.at[near(2), up_half], 1, behind)
    give(tk.at[near(3), down_half], tk.at[near(3), down_half], 1, ahead)
    sideways(near(2))
    sideways(near(3))
    forward(u_l, 8, 16, 2)
    forward(u_l, 0, 16, 1)

    def store_v(r, y):
        w_vg[pl.ds(r, 64, stride=16), :] = y

    def store_g(r, y):
        w_vg[pl.ds(8 + r, 64, stride=16), :] = y

    def store_f(r, y):
        w_f[pl.ds(r, 64, stride=8), :] = y

    inverse(0, 2, True, store_v)
    inverse(0, 1, False, store_g)
    for zz in range(8):
        s3[zz] = w_vg[zz * SIDE : (zz + 1) * SIDE].astype(BF16)
    for ds, mark in ((FAR, "f"), (CLOSE, "c")):
        for d in ds:
            peer = (z + d) % 8
            send(s3.at[peer], r3.at[z], "vz>", ">vz" + mark, along_z(peer))
    r3[pl.ds(z, 1)] = s3[pl.ds(z, 1)]
    inverse(1, 2, True, store_f)
    for zz in range(8):
        s3f[zz] = w_f[zz * 64 : (zz + 1) * 64].astype(BF16)

    arrived(tk.at[0], "tk>", ">tk1")
    sideways(near(6))
    arrived(r_c.at[0:7], "cq>", ">cq")
    wide_c[...] = r_c[...].astype(F32)

    def gate(at):
        x = r3[pl.ds(at, 1)].astype(F32).reshape(8, 16, SIDE)
        factor = wide_c[:, pl.ds(pl.multiple_of(at * 8, 8), 8), :]
        x = jnp.concatenate([x[:, :8], x[:, 8:] * factor], axis=1)
        r3[pl.ds(at, 1)] = x.astype(BF16).reshape(1, SIDE, SIDE)

    gate(z)
    send(r3.at[z], r3s.at[z], "sib>", ">sibc", (i, sib))
    for ds, mark in ((CLOSE, "c"), (FAR, "f")):
        arrived(r3.at[0 : len(ds)], "vz>", ">vz" + mark)
        for d in ds:
            peer = (z + d) % 8
            gate(peer)
            send(r3.at[peer], r3s.at[peer], "sib>", ">sib" + mark, (i, sib))
    for d in ORDER:
        peer = (q + d) % 8
        send(rows16(r3, peer), r4.at[q], "vq>", ">vq", along_q(peer))
    r4[pl.ds(q, 1)] = r3[:, pl.ds(pl.multiple_of(q * 16, 16), 16), :].reshape(1, 8, 16, SIDE)

    for d in ORDER:
        peer = (z + d) % 8
        send(s3f.at[peer], r3f.at[z], "fz>", ">fz", along_z(peer))
    r3f[pl.ds(z, 1)] = s3f[pl.ds(z, 1)]

    for qq in range(8):
        g_all[0:SIDE, qq * SIDE : (qq + 1) * SIDE] = r3[:, qq * 16 : (qq + 1) * 16, :].reshape(SIDE, SIDE)
    arrived(tk.at[0:3], "tk>", ">tk2")
    own.wait()
    arrived(r3s.at[0:5], "sib>", ">sibc")
    arrived(r3s.at[0:3], "sib>", ">sibf")
    for qq in range(8):
        g_all[SIDE:, qq * SIDE : (qq + 1) * SIDE] = r3s[:, qq * 16 : (qq + 1) * 16, :].reshape(SIDE, SIDE)
    for t in range(4):
        sums = dot(g_all[...], tk[:, :, t * 256 : (t + 1) * 256].reshape(1024, 256)).reshape(2, 8, 2, 8, 256)
        to = core * 4 + t
        for s, who in enumerate((c, sib)):
            rows = [sums[s, :, f].reshape(64, 256) for f in range(2)]
            at = (2 * t + s) * 8
            part[at : at + 8] = jnp.concatenate(rows, axis=0).T.astype(BF16).reshape(8, 32, SIDE)

            def share(slot, at=at, to=to, who=who):
                peer = near(slot)
                send(part.at[at + peer], r5.at[z * 8 + q], "rs>", ">rs", (to * 8 + peer, who))

            if s == 1:
                share(0)
            else:

                @pl.when(to != z)
                def _(share=share):
                    share(0)

                @pl.when(to == z)
                def _(at=at):
                    pltpu.make_async_copy(part.at[at + q], r5.at[z * 8 + q], sem("self")).start()

            for slot in range(1, 8):
                share(slot)

    arrived(r4.at[0:7], "vq>", ">vq")
    for qq in range(8):
        x = r4[qq].astype(F32)
        vt[:, qq * 64 : (qq + 1) * 64] = x[:, :8].reshape(64, SIDE).T.astype(BF16)
        gt[:, qq * 64 : (qq + 1) * 64] = x[:, 8:].reshape(64, SIDE).T.astype(BF16)

    def columns(k):
        rows = pl.ds(pl.multiple_of(k * 512, 512), 512)
        over = (((1,), (1,)), ((), ()))
        a = lax.dot_general(vt[...], vw[rows, :], over, preferred_element_type=F32)
        return a + lax.dot_general(gt[...], gw[rows, :], over, preferred_element_type=F32)

    s7[0] = columns(2 * (1 - xh) + 1 - core)
    s7[1] = columns(2 * xh + 1 - core)
    send(s7, r7, "core>", ">core", (i, sib))
    far = columns(2 * (1 - xh) + core)
    here = columns(2 * xh + core)
    arrived(r7, "core>", ">core")
    s8[...] = (far + r7[0]).astype(BF16)
    send(s8, r8, "far>", ">far", (i, opp))
    here = here + r7[1]

    arrived(r3f.at[0:7], "fz>", ">fz")
    regroup(r3f, s4f)
    for d in ORDER:
        peer = (q + d) % 8
        send(s4f.at[peer], r4f.at[q], "fq>", ">fq", along_q(peer))
    r4f[pl.ds(q, 1)] = s4f[pl.ds(q, 1)]

    outs = [
        pltpu.make_async_copy(a, b, sem(f"out{t}"))
        for t, (a, b) in enumerate(zip((o_in, o_fil), (input_grad, filter_grad)))
    ]
    arrived(r8, "far>", ">far")
    o_in[...] = (here + r8[...].astype(F32)).astype(BF16)
    outs[0].start()
    arrived(r4f.at[0:7], "fq>", ">fq")
    for b in range(4):
        x = r4f[2 * b : 2 * b + 2].astype(F32).reshape(SIDE, SIDE)
        o_fil[:, b * SIDE : (b + 1) * SIDE] = x.T * SCALE
    outs[1].start()

    @pl.when(core == z // 4)
    def _():
        waiter(r5.at[0:63], "rs>", ">rs").wait()
        pltpu.make_async_copy(part.at[0], r5.at[0], sem("self")).wait()

    @pl.when(core != z // 4)
    def _():
        waiter(r5, "rs>", ">rs").wait()

    for size, out in (
        (r1_e.at[0:7], "ez>"), (r2_e.at[0:7], "eq>"), (r1_l.at[0:7], "lq>"), (r2_l.at[0:7], "lz>"),
        (r3.at[0:7], "vz>"), (r_c.at[0:7], "cq>"), (r3s, "sib>"), (r3f.at[0:7], "fz>"), (r4.at[0:7], "vq>"), (r4f.at[0:7], "fq>"),
        (tk.at[0:7], "tk>"), (r7, "core>"), (r8, "far>"),
    ):
        waiter(size, out, ">ez").wait_send()
    for copy in outs:
        copy.wait()


def local(tokens, value_weight, gate_weight, filters, cotangent):
    def v(*shape, dtype=BF16):
        return pltpu.VMEM(shape, dtype)

    whole = pl.BlockSpec(memory_space=pl.ANY)
    operands = [tokens, value_weight, gate_weight, filters, cotangent]
    operands += [jnp.asarray(t) for t in tables()]
    shape = jax.ShapeDtypeStruct
    input_grad, filter_grad = shape((128, 512), BF16), shape((128, 512), F32)
    weight_grad, terms = shape((32, 512), F32), shape((64, 32, 128), BF16)
    results = pl.pallas_call(
        kernel,
        out_shape=(input_grad, filter_grad, terms),
        in_specs=[whole] * 9,
        out_specs=(whole,) * 3,
        scratch_shapes=[pltpu.VMEM(t.shape, t.dtype) for t in operands] + [
            v(128, 128), v(4, 256, 256), v(64, 384),
            v(8, 64, 128), v(8, 128, 128), v(8, 64, 128), v(8, 128, 128),
            v(8, 64, 128), v(8, 64, 128), v(8, 8, 16, 128),
            v(512, 128, dtype=F32), v(1024, 128, dtype=F32), v(1024, 128, dtype=F32), v(512, 128, dtype=F32),
            v(8, 64, 128), v(8, 64, 128), v(8, 64, 128, dtype=F32),
            v(3, 512, 256, dtype=F32), v(2, 512, 256), v(512, 256, dtype=F32),
            v(8, 128, 128), v(8, 128, 128), v(8, 128, 128), v(8, 8, 16, 128),
            v(8, 64, 128), v(8, 64, 128), v(8, 64, 128), v(8, 64, 128),
            v(8, 128, 1024), v(256, 1024), v(64, 32, 128),
            v(128, 512), v(128, 512),
            v(2, 128, 512, dtype=F32), v(2, 128, 512, dtype=F32), v(128, 512), v(128, 512),
        ] + [pltpu.VMEM(t.shape, t.dtype) for t in (input_grad, filter_grad)] + [pltpu.SemaphoreType.DMA((len(SEMAPHORES),))],
        compiler_params=pltpu.CompilerParams(
            collective_id=0, has_side_effects=True, vmem_limit_bytes=60 * 1024 * 1024
        ),
        cost_estimate=pl.CostEstimate(flops=3_000_000_000, bytes_accessed=8_000_000, transcendentals=0),
    )(*operands)
    outputs = (input_grad, filter_grad, weight_grad, weight_grad)
    return pl.pallas_call(
        finish,
        out_shape=outputs,
        in_specs=[whole] * 3,
        out_specs=(whole,) * 4,
        scratch_shapes=[pltpu.VMEM(t.shape, t.dtype) for t in outputs + (terms,)] + [pltpu.SemaphoreType.DMA((7,))],
        compiler_params=pltpu.CompilerParams(vmem_limit_bytes=60 * 1024 * 1024),
    )(*results)


def finish(
    in_grad_in, filter_grad_in, terms_in, in_grad, filter_grad, vw_grad, gw_grad,
    o_in, o_fil, o_vw, o_gw, terms, sems,
):
    loads = [
        pltpu.make_async_copy(a, b, sems.at[t])
        for t, (a, b) in enumerate(((terms_in, terms), (in_grad_in, o_in), (filter_grad_in, o_fil)))
    ]
    for load in loads:
        load.start()
    stores = [
        pltpu.make_async_copy(a, b, sems.at[3 + t])
        for t, (a, b) in enumerate(((o_in, in_grad), (o_fil, filter_grad), (o_vw, vw_grad), (o_gw, gw_grad)))
    ]
    loads[0].wait()
    for qq in range(8):
        total = terms[qq].astype(F32)
        for zz in range(1, 8):
            total = total + terms[zz * 8 + qq].astype(F32)
        total = total * SCALE
        o_vw[:, qq * 64 : (qq + 1) * 64] = total[:, :64]
        o_gw[:, qq * 64 : (qq + 1) * 64] = total[:, 64:]
    stores[2].start()
    stores[3].start()
    for t in (1, 2):
        loads[t].wait()
        stores[t - 1].start()
    for store in stores:
        store.wait()


def solution(mesh):
    placed = (P("seq", None), P(None, "ch"), P(None, "ch"), P("seq", "ch"), P("seq", "ch"))
    return jax.shard_map(
        local,
        mesh=mesh,
        in_specs=placed,
        out_specs=(P("seq", "ch"),) * 4,
        check_vma=False,
    )
```
